512 devices in a mesh: ctx: 32 (over y, x, core), head: 16 (over z).
Axes of the slice: x: 4, y: 4, z: 16, core: 2. Of those that a mesh axis runs over, the one named last changes fastest.
Arguments:
- queries: bfloat16 [8192, 4096], P('ctx', 'head'), may hold values from -50 to 50
- keys: bfloat16 [8192, 4096], P('ctx', 'head'), may hold values from -9 to 9
- values: bfloat16 [8192, 4096], P('ctx', 'head'), may hold values from -9 to 9
- near_blocks: int32 [64, 4], P('ctx'), may hold values from 0 to 63, as said below
- near_count: int32 [64], P('ctx'), may hold values from 1 to 4
- head_scale: float32 [32], P('head'), may hold values from 0.2 to 4.2
- gain: float32 [4096], P('head'), may hold values from 0.5 to 1.5
- cotangent: bfloat16 [8192, 4096], P('ctx', 'head'), may hold values from -6 to 6
Outputs:
- mixed: bfloat16 [8192, 4096], P('ctx', 'head')
- grad_queries: bfloat16 [8192, 4096], P('ctx', 'head')
- grad_keys: bfloat16 [8192, 4096], P('ctx', 'head')
- grad_values: bfloat16 [8192, 4096], P('ctx', 'head')
The draws below stay inside these ranges and needn't reach their ends.
Inputs may be any that keep to these rules, and one draw needn't show every extreme that they name: near_blocks[b, 0] = b; entries 1 to near_count[b] - 1 are distinct blocks other than b within 2 blocks of b; the later entries equal b.
All inputs are finite; a program needn't handle non-finite values.
Results may differ from the reference program's by a relative error of at most 0.022.
Values may be sent and summed in bfloat16 or wider, within the bound.
A program may use at most 64 MiB of HBM per device.

```python
import math
import jax
import jax.numpy as jnp
from jax import lax

HEADS = 32
HEAD_SIZE = 128
D = 4096
TOK_DEV = 256
TOKENS = 8192
BLOCK_TOKENS = 128
NBLK = 64
NEAR_SLOTS = 4
RB = 2
LEV = 5
N_CTX = 32


def token_and_window(key, salt):
    key_token = jax.random.fold_in(key, salt)
    key_window = jax.random.fold_in(key, salt + 1)
    windows = TOKENS // 2 ** LEV
    token_part = 0.6 * jax.random.truncated_normal(key_token, -6.0, 6.0, (TOKENS, D), jnp.float32)
    window_part = 0.8 * jax.random.truncated_normal(key_window, -6.0, 6.0, (windows, D), jnp.float32)
    return token_part + jnp.repeat(window_part, 2 ** LEV, axis=0)


def query_key_pair(key):
    key_query = jax.random.fold_in(key, 101)
    keys_drawn = token_and_window(key, 202)
    query_drawn = 2.5 * jax.random.truncated_normal(key_query, -6.0, 6.0, (TOKENS, D), jnp.float32)
    return (query_drawn, keys_drawn)


def draw_queries(key, part):
    return query_key_pair(key)[0].astype(jnp.bfloat16)


def draw_keys(key, part):
    return query_key_pair(key)[1].astype(jnp.bfloat16)


def draw_values(key, part):
    return token_and_window(key, 404).astype(jnp.bfloat16)


def near_lists(key):
    key_count = jax.random.fold_in(key, 7)
    key_order = jax.random.fold_in(key, 8)
    blocks = jnp.arange(NBLK, dtype=jnp.int32)
    offsets = jnp.concatenate([jnp.arange(-RB, 0, dtype=jnp.int32), jnp.arange(1, RB + 1, dtype=jnp.int32)])
    target = blocks[:, None] + offsets[None, :]
    inside = (target >= 0) & (target < NBLK)
    ranking = jax.random.randint(key_order, (NBLK, 2 * RB), 0, 1 << 20) * (2 * RB) + jnp.arange(2 * RB, dtype=jnp.int32)[None, :]
    ranking = ranking + jnp.where(inside, 0, 1 << 26)
    order = jnp.argsort(ranking, axis=1)
    chosen = jnp.take_along_axis(target, order, axis=1)[:, :NEAR_SLOTS - 1]
    available = 1 + jnp.sum(inside.astype(jnp.int32), axis=1)
    counts = jax.random.randint(key_count, (NBLK,), 1, NEAR_SLOTS + 1)
    counts = jnp.where(blocks % 7 == 3, NEAR_SLOTS, counts)
    counts = jnp.minimum(counts, available).astype(jnp.int32)
    lists = jnp.concatenate([blocks[:, None], chosen], axis=1)
    slots = jnp.arange(NEAR_SLOTS, dtype=jnp.int32)[None, :]
    lists = jnp.where(slots < counts[:, None], lists, blocks[:, None]).astype(jnp.int32)
    return (lists, counts)


def draw_near_blocks(key, part):
    return near_lists(key)[0]


def draw_near_count(key, part):
    return near_lists(key)[1]


def draw_head_scale(key, part):
    position = jnp.arange(HEADS, dtype=jnp.float32) / (HEADS - 1)
    base = 0.3 * jnp.power(10.0, position)
    jitter = jax.random.uniform(key, (HEADS,), jnp.float32, 0.85, 1.15)
    return (base * jitter).astype(jnp.float32)


def block_scale(own_key, shape, split, smallest, top_value):
    def one(dim, shards_of):
        draws = jax.random.uniform(jax.random.fold_in(jax.random.fold_in(own_key, 6), dim), (shards_of,), jnp.float32, smallest / len(split), top_value / len(split))
        return jnp.repeat(jnp.exp(draws), shape[dim] // shards_of).reshape((-1,) + (1,) * (len(shape) - dim - 1))

    level = one(*split[0])
    for cut in split[1:]:
        level = level * one(*cut)
    return level


def gaussian(stream_key, extent, scale, most, cuts=(), kind=jnp.bfloat16):
    array = jax.random.normal(stream_key, extent, jnp.float32) * scale
    if len(cuts) > 0:
        array = block_scale(stream_key, extent, cuts, -0.22, 0.18) * array
    return jnp.clip(array, min=-most, max=most).astype(kind)


def setup_inputs(seed: int = 0) -> dict:
    seeds = jax.random.split(jax.random.key(seed), 9)
    queries = draw_queries(jax.random.fold_in(seeds[8], 71), 0)
    keys = draw_keys(jax.random.fold_in(seeds[8], 71), 0)
    values = draw_values(jax.random.fold_in(seeds[8], 71), 0)
    near_blocks = draw_near_blocks(jax.random.fold_in(seeds[8], 71), 0)
    near_count = draw_near_count(jax.random.fold_in(seeds[8], 71), 0)
    head_scale = draw_head_scale(jax.random.fold_in(seeds[8], 71), 0)
    gain = jnp.clip(1.0 + 0.1 * jax.random.normal(seeds[6], (D,), jnp.float32), 0.5, 1.5)
    cotangent = gaussian(seeds[7], (TOKENS, D), 1.0, 6.0, ((0, 32), (1, 16)))
    return {"queries": queries, "keys": keys, "values": values, "near_blocks": near_blocks, "near_count": near_count, "head_scale": head_scale, "gain": gain, "cotangent": cotangent}


LOG_TWO = 0.6931471805599453
NEG_BIG = -1e+30
NORM_EPS = 1e-05

def pool_rows(matrix, factor):
    return matrix.astype(jnp.float32).reshape(-1, factor, matrix.shape[1]).mean(axis=1).astype(jnp.bfloat16)

def reference(queries, keys, values, near_blocks, near_count, head_scale, gain, cotangent):
    softmax_scale = 1.0 / math.sqrt(HEAD_SIZE)
    width = HEADS * HEAD_SIZE
    every_token = queries.shape[0]
    every_block = every_token // BLOCK_TOKENS
    valid = jnp.arange(NEAR_SLOTS, dtype=jnp.int32)[None, :] < near_count[:, None]
    key_mask = jnp.repeat(valid, BLOCK_TOKENS, axis=1)[:, None, :]
    plans = []
    for level_idx in range(LEV):
        factor = 2 ** (level_idx + 1)
        span = min(2 ** (level_idx + 1), N_CTX) * TOK_DEV
        plans.append((factor, span, span // factor))
    far_masks = []
    for level_idx in range(LEV):
        factor, span, per_group = plans[level_idx]
        groups = every_token // span
        q_pos = jnp.arange(every_token, dtype=jnp.int32).reshape(groups, span, 1)
        key_first = (jnp.arange(groups * per_group, dtype=jnp.int32) * factor).reshape(groups, 1, per_group)
        keep = jnp.abs(key_first // BLOCK_TOKENS - q_pos // BLOCK_TOKENS) > RB
        if level_idx > 0:
            prior = plans[level_idx - 1][1]
            keep = keep & (key_first // prior != q_pos // prior)
        far_masks.append(keep)
    pooled_keys = [pool_rows(keys, plan[0]) for plan in plans]
    pooled_values = [pool_rows(values, plan[0]) for plan in plans]
    flat_lists = near_blocks.reshape(-1)

    def head_cols(matrix, head):
        return lax.dynamic_slice_in_dim(matrix, head * HEAD_SIZE, HEAD_SIZE, 1)

    def forward_head(head):
        q_all = head_cols(queries, head)
        query_blocks = q_all.reshape(every_block, BLOCK_TOKENS, HEAD_SIZE).astype(jnp.float32)
        near_key_rows = head_cols(keys, head).reshape(every_block, BLOCK_TOKENS, HEAD_SIZE)[near_blocks].reshape(every_block, NEAR_SLOTS * BLOCK_TOKENS, HEAD_SIZE).astype(jnp.float32)
        near_value_rows = head_cols(values, head).reshape(every_block, BLOCK_TOKENS, HEAD_SIZE)[near_blocks].reshape(every_block, NEAR_SLOTS * BLOCK_TOKENS, HEAD_SIZE).astype(jnp.float32)
        near_score_rows = jnp.einsum('mne,mge->mng', query_blocks, near_key_rows) * softmax_scale
        near_score_rows = jnp.where(key_mask, near_score_rows, NEG_BIG)
        top = lax.optimization_barrier(jnp.max(near_score_rows, axis=2)).reshape(every_token)
        coarse_k = []
        coarse_v = []
        s_far = []
        for level_idx in range(LEV):
            factor, span, per_group = plans[level_idx]
            groups = every_token // span
            ck = head_cols(pooled_keys[level_idx], head).astype(jnp.float32).reshape(groups, per_group, HEAD_SIZE)
            cv = head_cols(pooled_values[level_idx], head).astype(jnp.float32).reshape(groups, per_group, HEAD_SIZE)
            q_group = q_all.astype(jnp.float32).reshape(groups, span, HEAD_SIZE)
            scores = jnp.einsum('gqd,gkd->gqk', q_group, ck) * softmax_scale + (level_idx + 1) * LOG_TWO
            scores = jnp.where(far_masks[level_idx], scores, NEG_BIG)
            coarse_k.append(ck)
            coarse_v.append(cv)
            s_far.append(scores)
            top = jnp.maximum(top, lax.optimization_barrier(jnp.max(scores, axis=2)).reshape(every_token))
        p_near = jnp.where(key_mask, jnp.exp(near_score_rows - top.reshape(every_block, BLOCK_TOKENS, 1)), 0.0)
        total = lax.optimization_barrier(jnp.sum(p_near, axis=2)).reshape(every_token)
        p_far = []
        for level_idx in range(LEV):
            factor, span, per_group = plans[level_idx]
            groups = every_token // span
            pf = jnp.where(far_masks[level_idx], jnp.exp(s_far[level_idx] - top.reshape(groups, span, 1)), 0.0)
            p_far.append(pf)
            total = total + lax.optimization_barrier(jnp.sum(pf, axis=2)).reshape(every_token)
        prob_near = p_near / total.reshape(every_block, BLOCK_TOKENS, 1)
        near_weight_rows = prob_near.astype(jnp.bfloat16)
        attention_output = jnp.einsum('itp,ipc->itc', near_weight_rows.astype(jnp.float32), near_value_rows).reshape(every_token, HEAD_SIZE)
        prob_far = []
        weight_far = []
        for level_idx in range(LEV):
            factor, span, per_group = plans[level_idx]
            groups = every_token // span
            pr = p_far[level_idx] / total.reshape(groups, span, 1)
            wf = pr.astype(jnp.bfloat16)
            prob_far.append(pr)
            weight_far.append(wf)
            attention_output = attention_output + jnp.einsum('gqk,gkd->gqd', wf.astype(jnp.float32), coarse_v[level_idx]).reshape(every_token, HEAD_SIZE)
        return (q_all, query_blocks, near_key_rows, near_value_rows, prob_near, near_weight_rows, coarse_k, coarse_v, prob_far, weight_far, attention_output)
    head_ids = jnp.arange(HEADS, dtype=jnp.int32)
    attn_all = lax.map(lambda head: forward_head(head)[10], head_ids)
    scale_cols = jnp.repeat(head_scale, HEAD_SIZE)[None, :]
    scaled = attn_all.transpose(1, 0, 2).reshape(every_token, width) * scale_cols
    inv = lax.rsqrt(lax.optimization_barrier(jnp.mean(scaled * scaled, axis=1)) + NORM_EPS)
    mixed = (scaled * inv[:, None] * gain[None, :]).astype(jnp.bfloat16)
    back = cotangent.astype(jnp.float32) * gain[None, :]
    inner = lax.optimization_barrier(jnp.mean(back * scaled, axis=1))
    d_scaled = inv[:, None] * (back - scaled * (inv * inv * inner)[:, None])
    d_attn = (d_scaled * scale_cols).astype(jnp.bfloat16)

    def backward_head(head):
        q_all, query_blocks, near_key_rows, near_value_rows, prob_near, near_weight_rows, coarse_k, coarse_v, prob_far, weight_far, attention_output = forward_head(head)
        d_out = head_cols(d_attn, head).astype(jnp.float32)
        delta = lax.optimization_barrier(jnp.sum(d_out * attention_output, axis=1))
        block_gradient = d_out.reshape(every_block, BLOCK_TOKENS, HEAD_SIZE)
        near_prob_gradient = jnp.einsum('mne,mge->mng', block_gradient, near_value_rows)
        near_score_gradient = (prob_near * (near_prob_gradient - delta.reshape(every_block, BLOCK_TOKENS, 1))).astype(jnp.bfloat16).astype(jnp.float32)
        query_gradient = jnp.einsum('itp,ipc->itc', near_score_gradient, near_key_rows).reshape(every_token, HEAD_SIZE)
        key_gradient_part = (jnp.einsum('ail,aiz->alz', near_score_gradient, query_blocks) * softmax_scale).reshape(every_block * NEAR_SLOTS, BLOCK_TOKENS, HEAD_SIZE)
        value_gradient_part = jnp.einsum('ail,aiz->alz', near_weight_rows.astype(jnp.float32), block_gradient).reshape(every_block * NEAR_SLOTS, BLOCK_TOKENS, HEAD_SIZE)
        grad_k = jnp.zeros((every_block, BLOCK_TOKENS, HEAD_SIZE), jnp.float32).at[flat_lists].add(key_gradient_part).reshape(every_token, HEAD_SIZE)
        grad_v = jnp.zeros((every_block, BLOCK_TOKENS, HEAD_SIZE), jnp.float32).at[flat_lists].add(value_gradient_part).reshape(every_token, HEAD_SIZE)
        for level_idx in range(LEV):
            factor, span, per_group = plans[level_idx]
            groups = every_token // span
            d_group = d_out.reshape(groups, span, HEAD_SIZE)
            q_group = q_all.astype(jnp.float32).reshape(groups, span, HEAD_SIZE)
            dp_far = jnp.einsum('gqd,gkd->gqk', d_group, coarse_v[level_idx])
            ds_far = (prob_far[level_idx] * (dp_far - delta.reshape(groups, span, 1))).astype(jnp.bfloat16).astype(jnp.float32)
            query_gradient = query_gradient + jnp.einsum('gqk,gkd->gqd', ds_far, coarse_k[level_idx]).reshape(every_token, HEAD_SIZE)
            dkc = (jnp.einsum('gqk,gqd->gkd', ds_far, q_group) * softmax_scale).reshape(every_token // factor, HEAD_SIZE)
            dvc = jnp.einsum('gqk,gqd->gkd', weight_far[level_idx].astype(jnp.float32), d_group).reshape(every_token // factor, HEAD_SIZE)
            grad_k = grad_k + jnp.repeat(dkc / factor, factor, axis=0)
            grad_v = grad_v + jnp.repeat(dvc / factor, factor, axis=0)
        return (query_gradient * softmax_scale, grad_k, grad_v)
    grad_q_all, grad_k_all, grad_v_all = lax.map(backward_head, head_ids)
    grad_queries = grad_q_all.transpose(1, 0, 2).reshape(every_token, width).astype(jnp.bfloat16)
    grad_keys = grad_k_all.transpose(1, 0, 2).reshape(every_token, width).astype(jnp.bfloat16)
    grad_values = grad_v_all.transpose(1, 0, 2).reshape(every_token, width).astype(jnp.bfloat16)
    return (mixed, grad_queries, grad_keys, grad_values)
```

```python
import functools
import math

import jax
import jax.numpy as jnp
from jax import lax
from jax.experimental import pallas as pl
from jax.experimental.pallas import tpu as pltpu
from jax.sharding import PartitionSpec as P

HS = 128
BT = 128
SLOTS = 4
NEG_BIG = -1e30
NORM_EPS = 1e-05
LOG2E = 1.4426950408889634
SCALE = 1.0 / math.sqrt(HS)
TOK = 256
COLS = 512
NEAR = 768
ROWS = 1408
COARSE = ROWS - NEAR
F32 = jnp.float32
BF16 = jnp.bfloat16


def dot(a, b, ca, cb):
    return lax.dot_general(
        a, b, (((ca,), (cb,)), ((), ())), preferred_element_type=F32
    )


def iota(shape, dim):
    return lax.broadcasted_iota(jnp.int32, shape, dim)


def pool_matrix(rows, level):
    hit = (iota((rows, TOK), 1) >> level) == iota((rows, TOK), 0)
    return jnp.where(hit, 2.0**-level, 0.0)


def kernel(
    n_ctx, n_head,
    q_hbm, k_hbm, v_hbm, nb_ref, nc_ref, hs_ref, gain_ref, cot_hbm,
    mixed_hbm, gq_hbm, gk_hbm, gv_hbm,
    kall, qv, cotv, pool, pool5, buf5, ps_own, ps_buf, cbias, back,
    pt, dst, cg, ext, c_send, c_recv, rim_out, rim_in, csum, csum5, ret, ret5,
    mixed_v, gq_v, gk_v, gv_v,
    ld_sem, out_sem, pool_send, pool_recv, fwd_send, fwd_recv, near_send, near_recv,
    ps_sem, cp_sem, rim_send, rim_recv, ret_send, ret_recv,
):
    d = lax.axis_index("ctx")
    z = lax.axis_index("head")
    n_chip = n_ctx // 2
    chip = lax.div(d, 2)
    core = lax.rem(d, 2)
    partner = chip * 2 + 1 - core
    other = lax.rem(d + n_ctx - 1 + 2 * core, n_ctx)
    width = float(n_head * 2 * HS)

    barrier = pltpu.get_barrier_semaphore()

    def hello(ctx, head):
        pl.semaphore_signal(
            barrier, inc=1, device_id=(ctx, head), device_id_type=pl.DeviceIdType.MESH
        )

    for m in range(1, n_head):
        hello(d, lax.rem(z + m, n_head))
    for m in range(1, n_chip):
        hello(lax.rem(chip + m, n_chip) * 2 + core, z)
    hello(other, z)
    hello(partner, z)

    def remote(src, dst_ref, ssem, rsem, ctx, head):
        return pltpu.make_async_remote_copy(
            src_ref=src, dst_ref=dst_ref, send_sem=ssem, recv_sem=rsem,
            device_id=(ctx, head), device_id_type=pl.DeviceIdType.MESH,
        )

    def wait_bytes(ref, sem):
        pltpu.make_async_copy(ref, ref, sem).wait()

    loads = [
        pltpu.make_async_copy(k_hbm, kall.at[pl.ds(TOK, TOK), pl.ds(0, 256)], ld_sem.at[0]),
        pltpu.make_async_copy(v_hbm, kall.at[pl.ds(TOK, TOK), pl.ds(256, 256)], ld_sem.at[1]),
        pltpu.make_async_copy(q_hbm, qv, ld_sem.at[2]),
        pltpu.make_async_copy(cot_hbm, cotv, ld_sem.at[3]),
    ]
    for load in loads:
        load.start()
    loads[0].wait()
    loads[1].wait()

    pm = jnp.concatenate(
        [pool_matrix(64, 2), pool_matrix(32, 3), pool_matrix(16, 4), pool_matrix(8, 5),
         jnp.zeros((8, TOK), F32)], axis=0,
    ).astype(BF16)
    pooled = dot(pm, kall[TOK : 2 * TOK, :], 1, 0)
    pool[...] = pooled[0:112].astype(BF16)
    pool5[...] = jnp.concatenate([pooled[112:120, 0:256], pooled[112:120, 256:512]], axis=0).astype(BF16)

    pl.semaphore_wait(barrier, n_head - 1 + n_chip - 1 + 2)

    def level_peers(li):
        c = 1 << li
        half = lax.div(chip, c)
        base = (half + 1 - 2 * lax.rem(half, 2)) * c
        return c, 64 >> li, base, lax.rem(chip, c)

    pool_off = (0, 64, 96)
    for li in range(4):
        c, n, base, pos = level_peers(li)
        for j in range(c):
            if li < 3:
                src = pool.at[pl.ds(pool_off[li], n)]
                row = pl.multiple_of(NEAR + 128 * (li + 1) + core * 64 + pos * n, 16)
                dst_ref = kall.at[pl.ds(row, n)]
            else:
                src = pool5
                dst_ref = buf5.at[core * 8 + pos]
            remote(src, dst_ref, pool_send.at[li], pool_recv.at[li], (base + j) * 2 + core, z).start()

    own = kall.at[pl.ds(TOK, TOK)]
    near_p = remote(
        own, kall.at[pl.ds(pl.multiple_of(core * 512, 256), TOK)],
        near_send.at[0], near_recv.at[0], partner, z,
    )
    near_o = remote(
        own, kall.at[pl.ds(pl.multiple_of((1 - core) * 512, 256), TOK)],
        near_send.at[1], near_recv.at[1], other, z,
    )
    near_p.start()
    near_o.start()

    qb = lax.div(iota((128, TOK), 1), 128) + 2 * d
    r = iota((128, TOK), 0)
    kb = 2 * partner + (r >> 6)
    cbias[0:128] = jnp.where(jnp.abs(kb - qb) > 2, 1.0, NEG_BIG)
    for li in range(4):
        c, n, base, pos = level_peers(li)
        rr = r & 63
        chips = base + (rr >> (6 - li))
        first = (chips * 2 + (r >> 6)) * TOK + (rr & (n - 1)) * (4 << li)
        cbias[128 * (li + 1) : 128 * (li + 2)] = jnp.where(
            jnp.abs((first >> 7) - qb) > 2, float(li + 2), NEG_BIG
        )
    loads[3].wait()
    gain = gain_ref[...]
    back[...] = (cotv[...].astype(F32) * gain).T
    loads[2].wait()

    def half_ref(li, which):
        if li < 3:
            row = pl.multiple_of(NEAR + 128 * (li + 1) + which * 64, 64)
            return kall.at[pl.ds(row, 64)]
        return buf5.at[pl.ds(which * 8, 8)]

    fwds = []
    for li in range(4):
        mine = half_ref(li, core)
        wait_bytes(mine, pool_recv.at[li])
        fwd = remote(mine, mine, fwd_send.at[li], fwd_recv.at[li], partner, z)
        fwd.start()
        fwds.append(fwd)

    near_p.wait_recv()
    p1 = pool_matrix(128, 1).astype(BF16)
    part = kall[pl.ds(pl.multiple_of((1 - core) * 512, 256), TOK), :]
    kall[NEAR : NEAR + 128, :] = dot(p1, part, 1, 0).astype(BF16)

    for li in range(4):
        fwds[li].wait_recv()
    five = buf5[...].astype(F32)
    kall[ROWS - 128 : ROWS, 0:256] = five[:, 0:8, :].reshape(128, 256).astype(BF16)
    kall[ROWS - 128 : ROWS, 256:512] = five[:, 8:16, :].reshape(128, 256).astype(BF16)

    def kcols(h):
        return slice(h * HS, (h + 1) * HS)

    def vcols(h):
        return slice(256 + h * HS, 256 + (h + 1) * HS)

    def group(h, lo, hi, bias):
        s = dot(kall[lo:hi, kcols(h)], qv[:, kcols(h)], 1, 1) * (SCALE * LOG2E) + bias
        top = jnp.max(s, axis=0, keepdims=True)
        p = jnp.exp2(s - top)
        total = jnp.sum(p, axis=0, keepdims=True)
        pt[h, lo:hi, :] = p.astype(BF16)
        out = dot(kall[lo:hi, vcols(h)], pt[h, lo:hi, :], 0, 0)
        return top, total, out

    coarse = [group(h, NEAR, ROWS, cbias[...]) for h in range(2)]

    near_o.wait_recv()
    lane_block = lax.div(iota((1, TOK), 1), 128)
    rows_bias = []
    for e in range(6):
        vals = []
        for i in range(2):
            if e - i < 0 or e - i > 4:
                vals.append(NEG_BIG)
                continue
            want = 2 * d - 2 + e
            hit = jnp.int32(0)
            for j in range(SLOTS):
                ok = jnp.where(nb_ref[i, j] == want, 1, 0) * jnp.where(nc_ref[i] > j, 1, 0)
                hit = jnp.maximum(hit, ok)
            vals.append(jnp.where(hit > 0, 0.0, NEG_BIG))
        row = jnp.where(lane_block == 0, vals[0], vals[1])
        rows_bias.append(jnp.broadcast_to(row, (128, TOK)))
    nbias = jnp.concatenate(rows_bias, axis=0)
    near = [group(h, 0, NEAR, nbias) for h in range(2)]

    attn, alphas, scaled = [], [], []
    usum = jnp.zeros((1, TOK), F32)
    vsum = jnp.zeros((1, TOK), F32)
    for h in range(2):
        m1, t1, o1 = near[h]
        m2, t2, o2 = coarse[h]
        top = jnp.maximum(m1, m2)
        a1 = jnp.exp2(m1 - top)
        a2 = jnp.exp2(m2 - top)
        inv_total = 1.0 / (a1 * t1 + a2 * t2)
        a1 = a1 * inv_total
        a2 = a2 * inv_total
        out = o1 * a1 + o2 * a2
        sc = out * hs_ref[h]
        usum = usum + jnp.sum(sc * sc, axis=0, keepdims=True)
        vsum = vsum + jnp.sum(sc * back[kcols(h), :], axis=0, keepdims=True)
        attn.append(out)
        alphas.append((a1, a2))
        scaled.append(sc)
    ps_own[0:1, :] = usum
    ps_own[1:2, :] = vsum
    for m in range(1, n_head):
        remote(
            ps_own, ps_buf.at[m - 1], ps_sem.at[0], ps_sem.at[1], d, lax.rem(z + m, n_head)
        ).start()

    u = iota((TOK, TOK), 0)
    col = iota((TOK, TOK), 1)
    lvl = (col >> 6) + 2
    rel = (col & 63) & ((256 >> lvl) - 1)
    spread = jnp.where(
        (u >> lvl) == rel,
        jnp.where(lvl == 2, 0.25, jnp.where(lvl == 3, 0.125, jnp.where(lvl == 4, 0.0625, 0.03125))),
        0.0,
    ).astype(BF16)
    e1 = jnp.where(
        (iota((TOK, 128), 0) >> 1) == iota((TOK, 128), 1), 0.5, 0.0
    ).astype(BF16)

    wait_bytes(ps_buf, ps_sem.at[1])
    sums = ps_own[...] + jnp.sum(ps_buf[...], axis=0)
    inv = lax.rsqrt(sums[0:1, :] / width + NORM_EPS)
    fac = inv * inv * (sums[1:2, :] / width)

    d_group = []
    for h in range(2):
        d_attn = (inv * hs_ref[h]) * (back[kcols(h), :] - scaled[h] * fac)
        d_group.append([(d_attn * a).astype(BF16) for a in alphas[h]])

    def backward(h, g, lo, hi, keep, off):
        dg = d_group[h][g]
        delta = jnp.sum(dg.astype(F32) * attn[h], axis=0, keepdims=True)
        dp = dot(kall[lo:hi, vcols(h)], dg, 1, 0)
        pg = pt[h, lo:hi, :]
        ds = (pg.astype(F32) * (dp - delta)).astype(BF16)
        dst[h, lo:hi, :] = ds
        keep[:, kcols(h)] = dot(ds, qv[:, kcols(h)], 1, 0) * SCALE
        keep[:, vcols(h)] = dot(pg, dg, 1, 1)

    for h in range(2):
        backward(h, 1, NEAR, ROWS, cg, NEAR)
    for li in range(4):
        row = pl.multiple_of(128 * (li + 1) + (1 - core) * 64, 64)
        c_send[64 * li : 64 * (li + 1), :] = cg[pl.ds(row, 64), :].astype(BF16)
    swap = remote(c_send, c_recv, cp_sem.at[0], cp_sem.at[1], partner, z)
    swap.start()

    for h in range(2):
        backward(h, 0, 0, NEAR, ext, 0)
    rim_out[1] = ext[pl.ds(pl.multiple_of(core * 512, 256), TOK), :].astype(BF16)
    rim_o = remote(rim_out.at[1], rim_in.at[1], rim_send.at[1], rim_recv.at[1], other, z)
    rim_o.start()
    rim_out[0] = (
        ext[pl.ds(pl.multiple_of((1 - core) * 512, 256), TOK), :]
        + dot(e1, cg[0:128, :].astype(BF16), 1, 0)
    ).astype(BF16)
    rim_p = remote(rim_out.at[0], rim_in.at[0], rim_send.at[0], rim_recv.at[0], partner, z)
    rim_p.start()

    swap.wait_recv()
    for li in range(4):
        row = pl.multiple_of(128 * (li + 1) + core * 64, 64)
        total = cg[pl.ds(row, 64), :] + c_recv[64 * li : 64 * (li + 1), :].astype(F32)
        if li < 3:
            csum[64 * li : 64 * (li + 1), :] = total.astype(BF16)
        else:
            csum5[...] = jnp.concatenate(
                [total[:, 0:256].reshape(8, 8, 256), total[:, 256:512].reshape(8, 8, 256)], axis=1
            ).astype(BF16)
        c, n, base, pos = level_peers(li)
        for j in range(c):
            if li < 3:
                src = csum.at[pl.ds(64 * li + j * n, n)]
                dst_ref = ret.at[pl.ds(pl.multiple_of(64 * li + pos * n, 16), n)]
            else:
                src = csum5.at[j]
                dst_ref = ret5.at[pos]
            remote(src, dst_ref, ret_send.at[li], ret_recv.at[li], (base + j) * 2 + core, z).start()

    for h in range(2):
        mixed_v[:, kcols(h)] = ((scaled[h] * inv).T * gain[:, kcols(h)]).astype(BF16)
    out_m = pltpu.make_async_copy(mixed_v, mixed_hbm, out_sem.at[0])
    out_m.start()
    for h in range(2):
        gqt = dot(kall[:, kcols(h)], dst[h], 0, 0) * SCALE
        gq_v[:, kcols(h)] = gqt.T.astype(BF16)
    out_q = pltpu.make_async_copy(gq_v, gq_hbm, out_sem.at[1])
    out_q.start()

    rim_p.wait_recv()
    rim_o.wait_recv()
    grad = ext[TOK : 2 * TOK, :] + rim_in[0].astype(F32) + rim_in[1].astype(F32)
    for li in range(3):
        wait_bytes(ret.at[pl.ds(64 * li, 64)], ret_recv.at[li])
    wait_bytes(ret5, ret_recv.at[3])
    last = ret5[...].astype(F32)
    last = jnp.concatenate(
        [last[:, 0:8, :].reshape(64, 256), last[:, 8:16, :].reshape(64, 256)], axis=1
    ).astype(BF16)
    whole = jnp.concatenate([ret[...], last], axis=0)
    grad = grad + dot(spread, whole, 1, 0)
    gk_v[...] = grad[:, 0:256].astype(BF16)
    out_k = pltpu.make_async_copy(gk_v, gk_hbm, out_sem.at[2])
    out_k.start()
    gv_v[...] = grad[:, 256:512].astype(BF16)
    out_v = pltpu.make_async_copy(gv_v, gv_hbm, out_sem.at[3])
    out_v.start()

    for li in range(4):
        shape = ret.at[pl.ds(64 * min(li, 2), 64)] if li < 3 else ret5
        wait_bytes(shape, pool_send.at[li])
        wait_bytes(shape, ret_send.at[li])
        fwds[li].wait_send()
    near_p.wait_send()
    near_o.wait_send()
    wait_bytes(ps_buf, ps_sem.at[0])
    swap.wait_send()
    rim_p.wait_send()
    rim_o.wait_send()
    out_m.wait()
    out_q.wait()
    out_k.wait()
    out_v.wait()


def solution(mesh):
    n_ctx, n_head = mesh.shape["ctx"], mesh.shape["head"]
    anywhere = pl.BlockSpec(memory_space=pl.ANY)
    smem = pl.BlockSpec(memory_space=pltpu.SMEM)
    vmem = pl.BlockSpec(memory_space=pltpu.VMEM)
    dma = pltpu.SemaphoreType.DMA

    def body(queries, keys, values, near_blocks, near_count, head_scale, gain, cotangent):
        out = jax.ShapeDtypeStruct((TOK, 256), BF16)
        return pl.pallas_call(
            functools.partial(kernel, n_ctx, n_head),
            out_shape=(out, out, out, out),
            in_specs=[anywhere, anywhere, anywhere, smem, smem, smem, vmem, anywhere],
            out_specs=(anywhere, anywhere, anywhere, anywhere),
            scratch_shapes=[
                pltpu.VMEM((ROWS, COLS), BF16),
                pltpu.VMEM((TOK, 256), BF16),
                pltpu.VMEM((TOK, 256), BF16),
                pltpu.VMEM((112, COLS), BF16),
                pltpu.VMEM((16, 256), BF16),
                pltpu.VMEM((16, 16, 256), BF16),
                pltpu.VMEM((2, TOK), F32),
                pltpu.VMEM((n_head - 1, 2, TOK), F32),
                pltpu.VMEM((COARSE, TOK), F32),
                pltpu.VMEM((256, TOK), F32),
                pltpu.VMEM((2, ROWS, TOK), BF16),
                pltpu.VMEM((2, ROWS, TOK), BF16),
                pltpu.VMEM((COARSE, COLS), F32),
                pltpu.VMEM((NEAR, COLS), F32),
                pltpu.VMEM((256, COLS), BF16),
                pltpu.VMEM((256, COLS), BF16),
                pltpu.VMEM((2, TOK, COLS), BF16),
                pltpu.VMEM((2, TOK, COLS), BF16),
                pltpu.VMEM((192, COLS), BF16),
                pltpu.VMEM((8, 16, 256), BF16),
                pltpu.VMEM((192, COLS), BF16),
                pltpu.VMEM((8, 16, 256), BF16),
                pltpu.VMEM((TOK, 256), BF16),
                pltpu.VMEM((TOK, 256), BF16),
                pltpu.VMEM((TOK, 256), BF16),
                pltpu.VMEM((TOK, 256), BF16),
                dma((4,)), dma((4,)), dma((4,)), dma((4,)), dma((4,)), dma((4,)),
                dma((2,)), dma((2,)), dma((2,)), dma((2,)), dma((2,)), dma((2,)),
                dma((4,)), dma((4,)),
            ],
            compiler_params=pltpu.CompilerParams(
                collective_id=0, has_side_effects=True, vmem_limit_bytes=40 * 1024 * 1024
            ),
        )(queries, keys, values, near_blocks, near_count, head_scale, gain.reshape(1, 256), cotangent)

    return jax.shard_map(
        body,
        mesh=mesh,
        in_specs=(
            P("ctx", "head"), P("ctx", "head"), P("ctx", "head"), P("ctx", None),
            P("ctx"), P("head"), P("head"), P("ctx", "head"),
        ),
        out_specs=(P("ctx", "head"), P("ctx", "head"), P("ctx", "head"), P("ctx", "head")),
        check_vma=False,
    )
```

```python
import functools
import math

import jax
import jax.numpy as jnp
from jax import lax
from jax.experimental import pallas as pl
from jax.experimental.pallas import tpu as pltpu
from jax.sharding import PartitionSpec as P

HS = 128
BT = 128
SLOTS = 4
NEG_BIG = -1e30
NORM_EPS = 1e-05
LOG2E = 1.4426950408889634
SCALE = 1.0 / math.sqrt(HS)
TOK = 256
COLS = 512
NEAR = 768
ROWS = 1408
COARSE = ROWS - NEAR
F32 = jnp.float32
BF16 = jnp.bfloat16


def dot(a, b, ca, cb):
    return lax.dot_general(
        a, b, (((ca,), (cb,)), ((), ())), preferred_element_type=F32
    )


def iota(shape, dim):
    return lax.broadcasted_iota(jnp.int32, shape, dim)


def pool_matrix(rows, level):
    hit = (iota((rows, TOK), 1) >> level) == iota((rows, TOK), 0)
    return jnp.where(hit, 2.0**-level, 0.0)


def kernel(
    n_ctx, n_head,
    q_hbm, k_hbm, v_hbm, nb_hbm, nc_hbm, hs_hbm, gain_hbm, cot_hbm,
    mixed_v, gq_v, gk_v, gv_v,
    nb_ref, nc_ref, hs_ref, gain_v,
    kall, qv, cotv, pool, pool5, buf5, ps_own, ps_buf, cbias, back,
    pt, dst, cg, ext, c_send, c_recv, rim_out, rim_in, csum, csum5, ret, ret5,
    ld_sem, pool_send, pool_recv, fwd_send, fwd_recv, near_send, near_recv,
    ps_sem, cp_sem, rim_send, rim_recv, ret_send, ret_recv,
):
    d = lax.axis_index("ctx")
    z = lax.axis_index("head")
    n_chip = n_ctx // 2
    chip = lax.div(d, 2)
    core = lax.rem(d, 2)
    partner = chip * 2 + 1 - core
    other = lax.rem(d + n_ctx - 1 + 2 * core, n_ctx)
    width = float(n_head * 2 * HS)

    barrier = pltpu.get_barrier_semaphore()

    def hello(ctx, head):
        pl.semaphore_signal(
            barrier, inc=1, device_id=(ctx, head), device_id_type=pl.DeviceIdType.MESH
        )

    for m in range(1, n_head):
        hello(d, lax.rem(z + m, n_head))
    for m in range(1, n_chip):
        hello(lax.rem(chip + m, n_chip) * 2 + core, z)
    hello(other, z)
    hello(partner, z)

    def remote(src, dst_ref, ssem, rsem, ctx, head):
        return pltpu.make_async_remote_copy(
            src_ref=src, dst_ref=dst_ref, send_sem=ssem, recv_sem=rsem,
            device_id=(ctx, head), device_id_type=pl.DeviceIdType.MESH,
        )

    def wait_bytes(ref, sem):
        pltpu.make_async_copy(ref, ref, sem).wait()

    loads = [
        pltpu.make_async_copy(k_hbm, kall.at[pl.ds(TOK, TOK), pl.ds(0, 256)], ld_sem.at[0]),
        pltpu.make_async_copy(v_hbm, kall.at[pl.ds(TOK, TOK), pl.ds(256, 256)], ld_sem.at[1]),
        pltpu.make_async_copy(q_hbm, qv, ld_sem.at[2]),
        pltpu.make_async_copy(cot_hbm, cotv, ld_sem.at[3]),
        pltpu.make_async_copy(gain_hbm, gain_v, ld_sem.at[4]),
        pltpu.make_async_copy(nb_hbm, nb_ref, ld_sem.at[5]),
        pltpu.make_async_copy(nc_hbm, nc_ref, ld_sem.at[6]),
        pltpu.make_async_copy(hs_hbm, hs_ref, ld_sem.at[7]),
    ]
    for load in loads:
        load.start()
    loads[0].wait()
    loads[1].wait()

    pm = jnp.concatenate(
        [pool_matrix(64, 2), pool_matrix(32, 3), pool_matrix(16, 4), pool_matrix(8, 5),
         jnp.zeros((8, TOK), F32)], axis=0,
    ).astype(BF16)
    pooled = dot(pm, kall[TOK : 2 * TOK, :], 1, 0)
    pool[...] = pooled[0:112].astype(BF16)
    pool5[...] = jnp.concatenate([pooled[112:120, 0:256], pooled[112:120, 256:512]], axis=0).astype(BF16)

    pl.semaphore_wait(barrier, n_head - 1 + n_chip - 1 + 2)

    def level_peers(li):
        c = 1 << li
        half = lax.div(chip, c)
        base = (half + 1 - 2 * lax.rem(half, 2)) * c
        return c, 64 >> li, base, lax.rem(chip, c)

    pool_off = (0, 64, 96)
    for li in range(4):
        c, n, base, pos = level_peers(li)
        for j in range(c):
            if li < 3:
                src = pool.at[pl.ds(pool_off[li], n)]
                row = pl.multiple_of(NEAR + 128 * (li + 1) + core * 64 + pos * n, 16)
                dst_ref = kall.at[pl.ds(row, n)]
            else:
                src = pool5
                dst_ref = buf5.at[core * 8 + pos]
            remote(src, dst_ref, pool_send.at[li], pool_recv.at[li], (base + j) * 2 + core, z).start()

    own = kall.at[pl.ds(TOK, TOK)]
    near_p = remote(
        own, kall.at[pl.ds(pl.multiple_of(core * 512, 256), TOK)],
        near_send.at[0], near_recv.at[0], partner, z,
    )
    near_o = remote(
        own, kall.at[pl.ds(pl.multiple_of((1 - core) * 512, 256), TOK)],
        near_send.at[1], near_recv.at[1], other, z,
    )
    near_p.start()
    near_o.start()

    qb = lax.div(iota((128, TOK), 1), 128) + 2 * d
    r = iota((128, TOK), 0)
    kb = 2 * partner + (r >> 6)
    cbias[0:128] = jnp.where(jnp.abs(kb - qb) > 2, 1.0, NEG_BIG)
    for li in range(4):
        c, n, base, pos = level_peers(li)
        rr = r & 63
        chips = base + (rr >> (6 - li))
        first = (chips * 2 + (r >> 6)) * TOK + (rr & (n - 1)) * (4 << li)
        cbias[128 * (li + 1) : 128 * (li + 2)] = jnp.where(
            jnp.abs((first >> 7) - qb) > 2, float(li + 2), NEG_BIG
        )
    loads[3].wait()
    loads[4].wait()
    gain = gain_v[...].reshape(1, 256)
    back[...] = (cotv[...].astype(F32) * gain).T
    for load in loads[5:]:
        load.wait()
    loads[2].wait()

    def half_ref(li, which):
        if li < 3:
            row = pl.multiple_of(NEAR + 128 * (li + 1) + which * 64, 64)
            return kall.at[pl.ds(row, 64)]
        return buf5.at[pl.ds(which * 8, 8)]

    fwds = []
    for li in range(4):
        mine = half_ref(li, core)
        wait_bytes(mine, pool_recv.at[li])
        fwd = remote(mine, mine, fwd_send.at[li], fwd_recv.at[li], partner, z)
        fwd.start()
        fwds.append(fwd)

    near_p.wait_recv()
    p1 = pool_matrix(128, 1).astype(BF16)
    part = kall[pl.ds(pl.multiple_of((1 - core) * 512, 256), TOK), :]
    kall[NEAR : NEAR + 128, :] = dot(p1, part, 1, 0).astype(BF16)

    for li in range(4):
        fwds[li].wait_recv()
    five = buf5[...].astype(F32)
    kall[ROWS - 128 : ROWS, 0:256] = five[:, 0:8, :].reshape(128, 256).astype(BF16)
    kall[ROWS - 128 : ROWS, 256:512] = five[:, 8:16, :].reshape(128, 256).astype(BF16)

    def kcols(h):
        return slice(h * HS, (h + 1) * HS)

    def vcols(h):
        return slice(256 + h * HS, 256 + (h + 1) * HS)

    def group(h, lo, hi, bias):
        s = dot(kall[lo:hi, kcols(h)], qv[:, kcols(h)], 1, 1) * (SCALE * LOG2E) + bias
        top = jnp.max(s, axis=0, keepdims=True)
        p = jnp.exp2(s - top)
        total = jnp.sum(p, axis=0, keepdims=True)
        pt[h, lo:hi, :] = p.astype(BF16)
        out = dot(kall[lo:hi, vcols(h)], pt[h, lo:hi, :], 0, 0)
        return top, total, out

    coarse = [group(h, NEAR, ROWS, cbias[...]) for h in range(2)]

    near_o.wait_recv()
    lane_block = lax.div(iota((1, TOK), 1), 128)
    rows_bias = []
    for e in range(6):
        vals = []
        for i in range(2):
            if e - i < 0 or e - i > 4:
                vals.append(NEG_BIG)
                continue
            want = 2 * d - 2 + e
            hit = jnp.int32(0)
            for j in range(SLOTS):
                ok = jnp.where(nb_ref[i, j] == want, 1, 0) * jnp.where(nc_ref[i] > j, 1, 0)
                hit = jnp.maximum(hit, ok)
            vals.append(jnp.where(hit > 0, 0.0, NEG_BIG))
        row = jnp.where(lane_block == 0, vals[0], vals[1])
        rows_bias.append(jnp.broadcast_to(row, (128, TOK)))
    nbias = jnp.concatenate(rows_bias, axis=0)
    near = [group(h, 0, NEAR, nbias) for h in range(2)]

    attn, alphas, scaled = [], [], []
    usum = jnp.zeros((1, TOK), F32)
    vsum = jnp.zeros((1, TOK), F32)
    for h in range(2):
        m1, t1, o1 = near[h]
        m2, t2, o2 = coarse[h]
        top = jnp.maximum(m1, m2)
        a1 = jnp.exp2(m1 - top)
        a2 = jnp.exp2(m2 - top)
        inv_total = 1.0 / (a1 * t1 + a2 * t2)
        a1 = a1 * inv_total
        a2 = a2 * inv_total
        out = o1 * a1 + o2 * a2
        sc = out * hs_ref[h]
        usum = usum + jnp.sum(sc * sc, axis=0, keepdims=True)
        vsum = vsum + jnp.sum(sc * back[kcols(h), :], axis=0, keepdims=True)
        attn.append(out)
        alphas.append((a1, a2))
        scaled.append(sc)
    ps_own[0:1, :] = usum
    ps_own[1:2, :] = vsum
    for m in range(1, n_head):
        remote(
            ps_own, ps_buf.at[m - 1], ps_sem.at[0], ps_sem.at[1], d, lax.rem(z + m, n_head)
        ).start()

    u = iota((TOK, TOK), 0)
    col = iota((TOK, TOK), 1)
    lvl = (col >> 6) + 2
    rel = (col & 63) & ((256 >> lvl) - 1)
    spread = jnp.where(
        (u >> lvl) == rel,
        jnp.where(lvl == 2, 0.25, jnp.where(lvl == 3, 0.125, jnp.where(lvl == 4, 0.0625, 0.03125))),
        0.0,
    ).astype(BF16)
    e1 = jnp.where(
        (iota((TOK, 128), 0) >> 1) == iota((TOK, 128), 1), 0.5, 0.0
    ).astype(BF16)

    wait_bytes(ps_buf, ps_sem.at[1])
    sums = ps_own[...] + jnp.sum(ps_buf[...], axis=0)
    inv = lax.rsqrt(sums[0:1, :] / width + NORM_EPS)
    fac = inv * inv * (sums[1:2, :] / width)

    d_group = []
    for h in range(2):
        d_attn = (inv * hs_ref[h]) * (back[kcols(h), :] - scaled[h] * fac)
        d_group.append([(d_attn * a).astype(BF16) for a in alphas[h]])

    def backward(h, g, lo, hi, keep, off):
        dg = d_group[h][g]
        delta = jnp.sum(dg.astype(F32) * attn[h], axis=0, keepdims=True)
        dp = dot(kall[lo:hi, vcols(h)], dg, 1, 0)
        pg = pt[h, lo:hi, :]
        ds = (pg.astype(F32) * (dp - delta)).astype(BF16)
        dst[h, lo:hi, :] = ds
        keep[:, kcols(h)] = dot(ds, qv[:, kcols(h)], 1, 0) * SCALE
        keep[:, vcols(h)] = dot(pg, dg, 1, 1)

    for h in range(2):
        backward(h, 1, NEAR, ROWS, cg, NEAR)
    for li in range(4):
        row = pl.multiple_of(128 * (li + 1) + (1 - core) * 64, 64)
        c_send[64 * li : 64 * (li + 1), :] = cg[pl.ds(row, 64), :].astype(BF16)
    swap = remote(c_send, c_recv, cp_sem.at[0], cp_sem.at[1], partner, z)
    swap.start()

    for h in range(2):
        backward(h, 0, 0, NEAR, ext, 0)
    rim_out[1] = ext[pl.ds(pl.multiple_of(core * 512, 256), TOK), :].astype(BF16)
    rim_o = remote(rim_out.at[1], rim_in.at[1], rim_send.at[1], rim_recv.at[1], other, z)
    rim_o.start()
    rim_out[0] = (
        ext[pl.ds(pl.multiple_of((1 - core) * 512, 256), TOK), :]
        + dot(e1, cg[0:128, :].astype(BF16), 1, 0)
    ).astype(BF16)
    rim_p = remote(rim_out.at[0], rim_in.at[0], rim_send.at[0], rim_recv.at[0], partner, z)
    rim_p.start()

    swap.wait_recv()
    for li in range(4):
        row = pl.multiple_of(128 * (li + 1) + core * 64, 64)
        total = cg[pl.ds(row, 64), :] + c_recv[64 * li : 64 * (li + 1), :].astype(F32)
        if li < 3:
            csum[64 * li : 64 * (li + 1), :] = total.astype(BF16)
        else:
            csum5[...] = jnp.concatenate(
                [total[:, 0:256].reshape(8, 8, 256), total[:, 256:512].reshape(8, 8, 256)], axis=1
            ).astype(BF16)
        c, n, base, pos = level_peers(li)
        for j in range(c):
            if li < 3:
                src = csum.at[pl.ds(64 * li + j * n, n)]
                dst_ref = ret.at[pl.ds(pl.multiple_of(64 * li + pos * n, 16), n)]
            else:
                src = csum5.at[j]
                dst_ref = ret5.at[pos]
            remote(src, dst_ref, ret_send.at[li], ret_recv.at[li], (base + j) * 2 + core, z).start()

    for h in range(2):
        mixed_v[:, kcols(h)] = ((scaled[h] * inv).T * gain[:, kcols(h)]).astype(BF16)
    for h in range(2):
        gqt = dot(kall[:, kcols(h)], dst[h], 0, 0) * SCALE
        gq_v[:, kcols(h)] = gqt.T.astype(BF16)

    rim_p.wait_recv()
    rim_o.wait_recv()
    grad = ext[TOK : 2 * TOK, :] + rim_in[0].astype(F32) + rim_in[1].astype(F32)
    for li in range(3):
        wait_bytes(ret.at[pl.ds(64 * li, 64)], ret_recv.at[li])
    wait_bytes(ret5, ret_recv.at[3])
    last = ret5[...].astype(F32)
    last = jnp.concatenate(
        [last[:, 0:8, :].reshape(64, 256), last[:, 8:16, :].reshape(64, 256)], axis=1
    ).astype(BF16)
    whole = jnp.concatenate([ret[...], last], axis=0)
    grad = grad + dot(spread, whole, 1, 0)
    gk_v[...] = grad[:, 0:256].astype(BF16)
    gv_v[...] = grad[:, 256:512].astype(BF16)

    for li in range(4):
        shape = ret.at[pl.ds(64 * min(li, 2), 64)] if li < 3 else ret5
        wait_bytes(shape, pool_send.at[li])
        wait_bytes(shape, ret_send.at[li])
        fwds[li].wait_send()
    near_p.wait_send()
    near_o.wait_send()
    wait_bytes(ps_buf, ps_sem.at[0])
    swap.wait_send()
    rim_p.wait_send()
    rim_o.wait_send()


def solution(mesh):
    n_ctx, n_head = mesh.shape["ctx"], mesh.shape["head"]
    hbm = pl.BlockSpec(memory_space=pl.ANY)
    vmem = pl.BlockSpec(memory_space=pltpu.VMEM)
    dma = pltpu.SemaphoreType.DMA

    def body(queries, keys, values, near_blocks, near_count, head_scale, gain, cotangent):
        out = jax.ShapeDtypeStruct((TOK, 256), BF16)
        outs = pl.pallas_call(
            functools.partial(kernel, n_ctx, n_head),
            out_shape=(out, out, out, out),
            in_specs=[hbm] * 8,
            out_specs=(vmem, vmem, vmem, vmem),
            scratch_shapes=[
                pltpu.SMEM((2, SLOTS), jnp.int32),
                pltpu.SMEM((2,), jnp.int32),
                pltpu.SMEM((2,), F32),
                pltpu.VMEM((256,), F32),
                pltpu.VMEM((ROWS, COLS), BF16),
                pltpu.VMEM((TOK, 256), BF16),
                pltpu.VMEM((TOK, 256), BF16),
                pltpu.VMEM((112, COLS), BF16),
                pltpu.VMEM((16, 256), BF16),
                pltpu.VMEM((16, 16, 256), BF16),
                pltpu.VMEM((2, TOK), F32),
                pltpu.VMEM((n_head - 1, 2, TOK), F32),
                pltpu.VMEM((COARSE, TOK), F32),
                pltpu.VMEM((256, TOK), F32),
                pltpu.VMEM((2, ROWS, TOK), BF16),
                pltpu.VMEM((2, ROWS, TOK), BF16),
                pltpu.VMEM((COARSE, COLS), F32),
                pltpu.VMEM((NEAR, COLS), F32),
                pltpu.VMEM((256, COLS), BF16),
                pltpu.VMEM((256, COLS), BF16),
                pltpu.VMEM((2, TOK, COLS), BF16),
                pltpu.VMEM((2, TOK, COLS), BF16),
                pltpu.VMEM((192, COLS), BF16),
                pltpu.VMEM((8, 16, 256), BF16),
                pltpu.VMEM((192, COLS), BF16),
                pltpu.VMEM((8, 16, 256), BF16),
                dma((8,)), dma((4,)), dma((4,)), dma((4,)), dma((4,)),
                dma((2,)), dma((2,)), dma((2,)), dma((2,)), dma((2,)), dma((2,)),
                dma((4,)), dma((4,)),
            ],
            compiler_params=pltpu.CompilerParams(
                collective_id=0, has_side_effects=True, vmem_limit_bytes=40 * 1024 * 1024
            ),
        )(queries, keys, values, near_blocks, near_count, head_scale, gain, cotangent)
        return outs

    return jax.shard_map(
        body,
        mesh=mesh,
        in_specs=(
            P("ctx", "head"), P("ctx", "head"), P("ctx", "head"), P("ctx", None),
            P("ctx"), P("head"), P("head"), P("ctx", "head"),
        ),
        out_specs=(P("ctx", "head"), P("ctx", "head"), P("ctx", "head"), P("ctx", "head")),
        check_vma=False,
    )
```

```python
import functools
import math

import jax
import jax.numpy as jnp
from jax import lax
from jax.experimental import pallas as pl
from jax.experimental.pallas import tpu as pltpu
from jax.sharding import PartitionSpec as P

HS = 128
BT = 128
SLOTS = 4
NEG_BIG = -1e30
NORM_EPS = 1e-05
LOG2E = 1.4426950408889634
SCALE = 1.0 / math.sqrt(HS)
TOK = 256
COLS = 512
NEAR = 768
ROWS = 1408
COARSE = ROWS - NEAR
F32 = jnp.float32
BF16 = jnp.bfloat16


def dot(a, b, ca, cb):
    return lax.dot_general(
        a, b, (((ca,), (cb,)), ((), ())), preferred_element_type=F32
    )


def iota(shape, dim):
    return lax.broadcasted_iota(jnp.int32, shape, dim)


def pool_matrix(rows, level):
    hit = (iota((rows, TOK), 1) >> level) == iota((rows, TOK), 0)
    return jnp.where(hit, 2.0**-level, 0.0)


def kernel(
    n_ctx, n_head,
    q_hbm, k_hbm, v_hbm, nb_hbm, nc_hbm, hs_hbm, gain_hbm, cot_hbm,
    mixed_v, gq_v, gk_v, gv_v,
    nb_ref, nc_ref, hs_ref, gain_v,
    kall, qv, cotv, pool, pool5, buf5, ps_own, ps_buf, cbias, back,
    pt, dst, cg, ext, c_send, c_recv, rim_out, rim_in, csum, csum5, ret, ret5,
    ld_sem, pool_send, pool_recv, fwd_send, fwd_recv, near_send, near_recv,
    ps_sem, cp_sem, rim_send, rim_recv, ret_send, ret_recv,
):
    d = lax.axis_index("ctx")
    z = lax.axis_index("head")
    n_chip = n_ctx // 2
    chip = lax.div(d, 2)
    core = lax.rem(d, 2)
    partner = chip * 2 + 1 - core
    other = lax.rem(d + n_ctx - 1 + 2 * core, n_ctx)
    width = float(n_head * 2 * HS)

    barrier = pltpu.get_barrier_semaphore()

    def hello(ctx, head):
        pl.semaphore_signal(
            barrier, inc=1, device_id=(ctx, head), device_id_type=pl.DeviceIdType.MESH
        )

    for m in range(1, n_head):
        hello(d, lax.rem(z + m, n_head))
    for m in range(1, n_chip):
        hello(lax.rem(chip + m, n_chip) * 2 + core, z)
    hello(other, z)
    hello(partner, z)

    def remote(src, dst_ref, ssem, rsem, ctx, head):
        return pltpu.make_async_remote_copy(
            src_ref=src, dst_ref=dst_ref, send_sem=ssem, recv_sem=rsem,
            device_id=(ctx, head), device_id_type=pl.DeviceIdType.MESH,
        )

    def wait_bytes(ref, sem):
        pltpu.make_async_copy(ref, ref, sem).wait()

    loads = [
        pltpu.make_async_copy(k_hbm, kall.at[pl.ds(TOK, TOK), pl.ds(0, 256)], ld_sem.at[0]),
        pltpu.make_async_copy(v_hbm, kall.at[pl.ds(TOK, TOK), pl.ds(256, 256)], ld_sem.at[1]),
        pltpu.make_async_copy(q_hbm, qv, ld_sem.at[2]),
        pltpu.make_async_copy(cot_hbm, cotv, ld_sem.at[3]),
        pltpu.make_async_copy(gain_hbm, gain_v, ld_sem.at[4]),
        pltpu.make_async_copy(nb_hbm, nb_ref, ld_sem.at[5]),
        pltpu.make_async_copy(nc_hbm, nc_ref, ld_sem.at[6]),
        pltpu.make_async_copy(hs_hbm, hs_ref, ld_sem.at[7]),
    ]
    for load in loads:
        load.start()
    loads[0].wait()
    loads[1].wait()

    pm = jnp.concatenate(
        [pool_matrix(64, 2), pool_matrix(32, 3), pool_matrix(16, 4), pool_matrix(8, 5),
         jnp.zeros((8, TOK), F32)], axis=0,
    ).astype(BF16)
    pooled = dot(pm, kall[TOK : 2 * TOK, :], 1, 0)
    pool[...] = pooled[0:112].astype(BF16)
    pool5[...] = jnp.concatenate([pooled[112:120, 0:256], pooled[112:120, 256:512]], axis=0).astype(BF16)

    pl.semaphore_wait(barrier, n_head - 1 + n_chip - 1 + 2)

    def level_peers(li):
        c = 1 << li
        half = lax.div(chip, c)
        base = (half + 1 - 2 * lax.rem(half, 2)) * c
        return c, 64 >> li, base, lax.rem(chip, c)

    pool_off = (0, 64, 96)
    for li in range(4):
        c, n, base, pos = level_peers(li)
        for j in range(c):
            if li < 3:
                src = pool.at[pl.ds(pool_off[li], n)]
                row = pl.multiple_of(NEAR + 128 * (li + 1) + core * 64 + pos * n, 16)
                dst_ref = kall.at[pl.ds(row, n)]
            else:
                src = pool5
                dst_ref = buf5.at[core * 8 + pos]
            remote(src, dst_ref, pool_send.at[li], pool_recv.at[li], (base + j) * 2 + core, z).start()

    own = kall.at[pl.ds(TOK, TOK)]
    near_p = remote(
        own, kall.at[pl.ds(pl.multiple_of(core * 512, 256), TOK)],
        near_send.at[0], near_recv.at[0], partner, z,
    )
    near_o = remote(
        own, kall.at[pl.ds(pl.multiple_of((1 - core) * 512, 256), TOK)],
        near_send.at[1], near_recv.at[1], other, z,
    )
    near_p.start()
    near_o.start()

    qb = lax.div(iota((128, TOK), 1), 128) + 2 * d
    r = iota((128, TOK), 0)
    kb = 2 * partner + (r >> 6)
    cbias[0:128] = jnp.where(jnp.abs(kb - qb) > 2, 1.0, NEG_BIG)
    for li in range(4):
        c, n, base, pos = level_peers(li)
        rr = r & 63
        chips = base + (rr >> (6 - li))
        first = (chips * 2 + (r >> 6)) * TOK + (rr & (n - 1)) * (4 << li)
        cbias[128 * (li + 1) : 128 * (li + 2)] = jnp.where(
            jnp.abs((first >> 7) - qb) > 2, float(li + 2), NEG_BIG
        )
    loads[3].wait()
    loads[4].wait()
    gain = gain_v[...].reshape(1, 256)
    back[...] = (cotv[...].astype(F32) * gain).T
    for load in loads[5:]:
        load.wait()
    loads[2].wait()

    def half_ref(li, which):
        if li < 3:
            row = pl.multiple_of(NEAR + 128 * (li + 1) + which * 64, 64)
            return kall.at[pl.ds(row, 64)]
        return buf5.at[pl.ds(which * 8, 8)]

    fwds = []
    for li in range(4):
        mine = half_ref(li, core)
        wait_bytes(mine, pool_recv.at[li])
        fwd = remote(mine, mine, fwd_send.at[li], fwd_recv.at[li], partner, z)
        fwd.start()
        fwds.append(fwd)

    near_p.wait_recv()
    p1 = pool_matrix(128, 1).astype(BF16)
    part = kall[pl.ds(pl.multiple_of((1 - core) * 512, 256), TOK), :]
    kall[NEAR : NEAR + 128, :] = dot(p1, part, 1, 0).astype(BF16)

    for li in range(4):
        fwds[li].wait_recv()
    five = buf5[...].astype(F32)
    kall[ROWS - 128 : ROWS, 0:256] = five[:, 0:8, :].reshape(128, 256).astype(BF16)
    kall[ROWS - 128 : ROWS, 256:512] = five[:, 8:16, :].reshape(128, 256).astype(BF16)

    def kcols(h):
        return slice(h * HS, (h + 1) * HS)

    def vcols(h):
        return slice(256 + h * HS, 256 + (h + 1) * HS)

    def group(h, lo, hi, bias):
        s = dot(kall[lo:hi, kcols(h)], qv[:, kcols(h)], 1, 1) * (SCALE * LOG2E) + bias
        top = jnp.max(s, axis=0, keepdims=True)
        p = jnp.exp2(s - top)
        total = jnp.sum(p, axis=0, keepdims=True)
        pt[h, lo:hi, :] = p.astype(BF16)
        out = dot(kall[lo:hi, vcols(h)], pt[h, lo:hi, :], 0, 0)
        return top, total, out

    coarse = [group(h, NEAR, ROWS, cbias[...]) for h in range(2)]

    near_o.wait_recv()
    lane_block = lax.div(iota((1, TOK), 1), 128)
    rows_bias = []
    for e in range(6):
        vals = []
        for i in range(2):
            if e - i < 0 or e - i > 4:
                vals.append(NEG_BIG)
                continue
            want = 2 * d - 2 + e
            hit = jnp.int32(0)
            for j in range(SLOTS):
                ok = jnp.where(nb_ref[i, j] == want, 1, 0) * jnp.where(nc_ref[i] > j, 1, 0)
                hit = jnp.maximum(hit, ok)
            vals.append(jnp.where(hit > 0, 0.0, NEG_BIG))
        row = jnp.where(lane_block == 0, vals[0], vals[1])
        rows_bias.append(jnp.broadcast_to(row, (128, TOK)))
    nbias = jnp.concatenate(rows_bias, axis=0)
    near = [group(h, 0, NEAR, nbias) for h in range(2)]

    attn, alphas, scaled = [], [], []
    usum = jnp.zeros((1, TOK), F32)
    vsum = jnp.zeros((1, TOK), F32)
    for h in range(2):
        m1, t1, o1 = near[h]
        m2, t2, o2 = coarse[h]
        top = jnp.maximum(m1, m2)
        a1 = jnp.exp2(m1 - top)
        a2 = jnp.exp2(m2 - top)
        inv_total = 1.0 / (a1 * t1 + a2 * t2)
        a1 = a1 * inv_total
        a2 = a2 * inv_total
        out = o1 * a1 + o2 * a2
        sc = out * hs_ref[h]
        usum = usum + jnp.sum(sc * sc, axis=0, keepdims=True)
        vsum = vsum + jnp.sum(sc * back[kcols(h), :], axis=0, keepdims=True)
        attn.append(out)
        alphas.append((a1, a2))
        scaled.append(sc)
    ps_own[0:1, :] = usum
    ps_own[1:2, :] = vsum
    for m in range(1, n_head):
        remote(
            ps_own, ps_buf.at[m - 1], ps_sem.at[0], ps_sem.at[1], d, lax.rem(z + m, n_head)
        ).start()

    u = iota((TOK, TOK), 0)
    col = iota((TOK, TOK), 1)
    lvl = (col >> 6) + 2
    rel = (col & 63) & ((256 >> lvl) - 1)
    spread = jnp.where(
        (u >> lvl) == rel,
        jnp.where(lvl == 2, 0.25, jnp.where(lvl == 3, 0.125, jnp.where(lvl == 4, 0.0625, 0.03125))),
        0.0,
    ).astype(BF16)
    e1 = jnp.where(
        (iota((TOK, 128), 0) >> 1) == iota((TOK, 128), 1), 0.5, 0.0
    ).astype(BF16)

    wait_bytes(ps_buf, ps_sem.at[1])
    sums = ps_own[...] + jnp.sum(ps_buf[...], axis=0)
    inv = lax.rsqrt(sums[0:1, :] / width + NORM_EPS)
    fac = inv * inv * (sums[1:2, :] / width)

    d_group = []
    for h in range(2):
        d_attn = (inv * hs_ref[h]) * (back[kcols(h), :] - scaled[h] * fac)
        d_group.append([(d_attn * a).astype(BF16) for a in alphas[h]])

    def backward(h, g, lo, hi, keep, off):
        dg = d_group[h][g]
        delta = jnp.sum(dg.astype(F32) * attn[h], axis=0, keepdims=True)
        dp = dot(kall[lo:hi, vcols(h)], dg, 1, 0)
        pg = pt[h, lo:hi, :]
        ds = (pg.astype(F32) * (dp - delta)).astype(BF16)
        dst[h, lo:hi, :] = ds
        keep[:, kcols(h)] = dot(ds, qv[:, kcols(h)], 1, 0) * SCALE
        keep[:, vcols(h)] = dot(pg, dg, 1, 1)

    for h in range(2):
        backward(h, 1, NEAR, ROWS, cg, NEAR)
    for li in range(4):
        row = pl.multiple_of(128 * (li + 1) + (1 - core) * 64, 64)
        c_send[64 * li : 64 * (li + 1), :] = cg[pl.ds(row, 64), :].astype(BF16)
    swap = remote(c_send, c_recv, cp_sem.at[0], cp_sem.at[1], partner, z)
    swap.start()

    for h in range(2):
        backward(h, 0, 0, NEAR, ext, 0)
    rim_out[1] = ext[pl.ds(pl.multiple_of(core * 512, 256), TOK), :].astype(BF16)
    rim_o = remote(rim_out.at[1], rim_in.at[1], rim_send.at[1], rim_recv.at[1], other, z)
    rim_o.start()
    rim_out[0] = (
        ext[pl.ds(pl.multiple_of((1 - core) * 512, 256), TOK), :]
        + dot(e1, cg[0:128, :].astype(BF16), 1, 0)
    ).astype(BF16)
    rim_p = remote(rim_out.at[0], rim_in.at[0], rim_send.at[0], rim_recv.at[0], partner, z)
    rim_p.start()

    swap.wait_recv()
    for li in range(4):
        row = pl.multiple_of(128 * (li + 1) + core * 64, 64)
        total = cg[pl.ds(row, 64), :] + c_recv[64 * li : 64 * (li + 1), :].astype(F32)
        if li < 3:
            csum[64 * li : 64 * (li + 1), :] = total.astype(BF16)
        else:
            csum5[...] = jnp.concatenate(
                [total[:, 0:256].reshape(8, 8, 256), total[:, 256:512].reshape(8, 8, 256)], axis=1
            ).astype(BF16)
        c, n, base, pos = level_peers(li)
        for j in range(c):
            if li < 3:
                src = csum.at[pl.ds(64 * li + j * n, n)]
                dst_ref = ret.at[pl.ds(pl.multiple_of(64 * li + pos * n, 16), n)]
            else:
                src = csum5.at[j]
                dst_ref = ret5.at[pos]
            remote(src, dst_ref, ret_send.at[li], ret_recv.at[li], (base + j) * 2 + core, z).start()

    for h in range(2):
        mixed_v[:, kcols(h)] = ((scaled[h] * inv).T * gain[:, kcols(h)]).astype(BF16)
    for h in range(2):
        gqt = dot(kall[:, kcols(h)], dst[h], 0, 0) * SCALE
        gq_v[:, kcols(h)] = gqt.T.astype(BF16)

    rim_p.wait_recv()
    rim_o.wait_recv()
    grad = ext[TOK : 2 * TOK, :] + rim_in[0].astype(F32) + rim_in[1].astype(F32)
    for li in range(3):
        wait_bytes(ret.at[pl.ds(64 * li, 64)], ret_recv.at[li])
    wait_bytes(ret5, ret_recv.at[3])
    last = ret5[...].astype(F32)
    last = jnp.concatenate(
        [last[:, 0:8, :].reshape(64, 256), last[:, 8:16, :].reshape(64, 256)], axis=1
    ).astype(BF16)
    whole = jnp.concatenate([ret[...], last], axis=0)
    grad = grad + dot(spread, whole, 1, 0)
    gk_v[...] = grad[:, 0:256].astype(BF16)
    gv_v[...] = grad[:, 256:512].astype(BF16)

    for li in range(4):
        shape = ret.at[pl.ds(64 * min(li, 2), 64)] if li < 3 else ret5
        wait_bytes(shape, pool_send.at[li])
        wait_bytes(shape, ret_send.at[li])
        fwds[li].wait_send()
    near_p.wait_send()
    near_o.wait_send()
    wait_bytes(ps_buf, ps_sem.at[0])
    swap.wait_send()
    rim_p.wait_send()
    rim_o.wait_send()


def store(a, b, c, e, a_hbm, b_hbm, c_hbm, e_hbm, sem):
    copies = [
        pltpu.make_async_copy(src, dst_ref, sem.at[i])
        for i, (src, dst_ref) in enumerate(((a, a_hbm), (b, b_hbm), (c, c_hbm), (e, e_hbm)))
    ]
    for copy in copies:
        copy.start()
    for copy in copies:
        copy.wait()


def solution(mesh):
    n_ctx, n_head = mesh.shape["ctx"], mesh.shape["head"]
    hbm = pl.BlockSpec(memory_space=pl.ANY)
    vmem = pl.BlockSpec(memory_space=pltpu.VMEM)
    dma = pltpu.SemaphoreType.DMA

    def body(queries, keys, values, near_blocks, near_count, head_scale, gain, cotangent):
        out = jax.ShapeDtypeStruct((TOK, 256), BF16)
        outs = pl.pallas_call(
            functools.partial(kernel, n_ctx, n_head),
            out_shape=(pltpu.VMEM((TOK, 256), BF16),) * 4,
            in_specs=[hbm] * 8,
            out_specs=(vmem, vmem, vmem, vmem),
            scratch_shapes=[
                pltpu.SMEM((2, SLOTS), jnp.int32),
                pltpu.SMEM((2,), jnp.int32),
                pltpu.SMEM((2,), F32),
                pltpu.VMEM((256,), F32),
                pltpu.VMEM((ROWS, COLS), BF16),
                pltpu.VMEM((TOK, 256), BF16),
                pltpu.VMEM((TOK, 256), BF16),
                pltpu.VMEM((112, COLS), BF16),
                pltpu.VMEM((16, 256), BF16),
                pltpu.VMEM((16, 16, 256), BF16),
                pltpu.VMEM((2, TOK), F32),
                pltpu.VMEM((n_head - 1, 2, TOK), F32),
                pltpu.VMEM((COARSE, TOK), F32),
                pltpu.VMEM((256, TOK), F32),
                pltpu.VMEM((2, ROWS, TOK), BF16),
                pltpu.VMEM((2, ROWS, TOK), BF16),
                pltpu.VMEM((COARSE, COLS), F32),
                pltpu.VMEM((NEAR, COLS), F32),
                pltpu.VMEM((256, COLS), BF16),
                pltpu.VMEM((256, COLS), BF16),
                pltpu.VMEM((2, TOK, COLS), BF16),
                pltpu.VMEM((2, TOK, COLS), BF16),
                pltpu.VMEM((192, COLS), BF16),
                pltpu.VMEM((8, 16, 256), BF16),
                pltpu.VMEM((192, COLS), BF16),
                pltpu.VMEM((8, 16, 256), BF16),
                dma((8,)), dma((4,)), dma((4,)), dma((4,)), dma((4,)),
                dma((2,)), dma((2,)), dma((2,)), dma((2,)), dma((2,)), dma((2,)),
                dma((4,)), dma((4,)),
            ],
            compiler_params=pltpu.CompilerParams(
                collective_id=0, has_side_effects=True, vmem_limit_bytes=56 * 1024 * 1024
            ),
        )(queries, keys, values, near_blocks, near_count, head_scale, gain, cotangent)
        return pl.pallas_call(
            store,
            out_shape=(out, out, out, out),
            in_specs=[hbm] * 4,
            out_specs=(hbm, hbm, hbm, hbm),
            scratch_shapes=[dma((4,))],
            compiler_params=pltpu.CompilerParams(vmem_limit_bytes=1024 * 1024),
        )(*outs)

    return jax.shard_map(
        body,
        mesh=mesh,
        in_specs=(
            P("ctx", "head"), P("ctx", "head"), P("ctx", "head"), P("ctx", None),
            P("ctx"), P("head"), P("head"), P("ctx", "head"),
        ),
        out_specs=(P("ctx", "head"), P("ctx", "head"), P("ctx", "head"), P("ctx", "head")),
        check_vma=False,
    )
```

```python
import functools
import math

import jax
import jax.numpy as jnp
from jax import lax
from jax.experimental import pallas as pl
from jax.experimental.pallas import tpu as pltpu
from jax.sharding import PartitionSpec as P

HS = 128
BT = 128
SLOTS = 4
NEG_BIG = -1e30
NORM_EPS = 1e-05
LOG2E = 1.4426950408889634
SCALE = 1.0 / math.sqrt(HS)
TOK = 256
COLS = 512
NEAR = 768
ROWS = 1408
COARSE = ROWS - NEAR
F32 = jnp.float32
BF16 = jnp.bfloat16


def dot(a, b, ca, cb):
    return lax.dot_general(
        a, b, (((ca,), (cb,)), ((), ())), preferred_element_type=F32
    )


def iota(shape, dim):
    return lax.broadcasted_iota(jnp.int32, shape, dim)


def pool_matrix(rows, level):
    hit = (iota((rows, TOK), 1) >> level) == iota((rows, TOK), 0)
    return jnp.where(hit, 2.0**-level, 0.0)


def kernel(
    n_ctx, n_head,
    q_hbm, k_hbm, v_hbm, nb_hbm, nc_hbm, hs_hbm, gain_hbm, cot_hbm,
    mixed_v, gq_v, gk_v, gv_v,
    nb_ref, nc_ref, hs_ref, gain_v,
    kall, qv, cotv, pool, pool5, buf5, ps_own, ps_buf, cbias, back,
    pt, dst, cg, ext, c_send, c_recv, rim_out, rim_in, csum, csum5, ret, ret5,
    ld_sem, pool_send, pool_recv, fwd_send, fwd_recv, near_send, near_recv,
    ps_sem, cp_sem, rim_send, rim_recv, ret_send, ret_recv,
):
    d = lax.axis_index("ctx")
    z = lax.axis_index("head")
    n_chip = n_ctx // 2
    chip = lax.div(d, 2)
    core = lax.rem(d, 2)
    across = 1 - core
    partner = chip * 2 + across
    other = lax.rem(d + n_ctx - 1 + 2 * core, n_ctx)
    width = float(n_head * 2 * HS)

    barrier = pltpu.get_barrier_semaphore()

    def hello(ctx, head):
        pl.semaphore_signal(
            barrier, inc=1, device_id=(ctx, head), device_id_type=pl.DeviceIdType.MESH
        )

    for m in range(1, n_head):
        hello(d, lax.rem(z + m, n_head))
    for m in range(1, n_chip):
        hello(lax.rem(chip + m, n_chip) * 2 + across, z)
    hello(partner, z)

    def remote(src, dst_ref, ssem, rsem, ctx, head):
        return pltpu.make_async_remote_copy(
            src_ref=src, dst_ref=dst_ref, send_sem=ssem, recv_sem=rsem,
            device_id=(ctx, head), device_id_type=pl.DeviceIdType.MESH,
        )

    def wait_bytes(ref, sem):
        pltpu.make_async_copy(ref, ref, sem).wait()

    loads = [
        pltpu.make_async_copy(k_hbm, kall.at[pl.ds(TOK, TOK), pl.ds(0, 256)], ld_sem.at[0]),
        pltpu.make_async_copy(v_hbm, kall.at[pl.ds(TOK, TOK), pl.ds(256, 256)], ld_sem.at[1]),
        pltpu.make_async_copy(q_hbm, qv, ld_sem.at[2]),
        pltpu.make_async_copy(cot_hbm, cotv, ld_sem.at[3]),
        pltpu.make_async_copy(gain_hbm, gain_v, ld_sem.at[4]),
        pltpu.make_async_copy(nb_hbm, nb_ref, ld_sem.at[5]),
        pltpu.make_async_copy(nc_hbm, nc_ref, ld_sem.at[6]),
        pltpu.make_async_copy(hs_hbm, hs_ref, ld_sem.at[7]),
    ]
    for load in loads:
        load.start()
    loads[0].wait()
    loads[1].wait()

    pm = jnp.concatenate(
        [pool_matrix(64, 2), pool_matrix(32, 3), pool_matrix(16, 4), pool_matrix(8, 5),
         jnp.zeros((8, TOK), F32)], axis=0,
    ).astype(BF16)
    pooled = dot(pm, kall[TOK : 2 * TOK, :], 1, 0)
    pool[...] = pooled[0:112].astype(BF16)
    pool5[...] = jnp.concatenate([pooled[112:120, 0:256], pooled[112:120, 256:512]], axis=0).astype(BF16)

    pl.semaphore_wait(barrier, n_head - 1 + n_chip - 1 + 1)

    def level_peers(li):
        c = 1 << li
        half = lax.div(chip, c)
        base = (half + 1 - 2 * lax.rem(half, 2)) * c
        return c, 64 >> li, base, lax.rem(chip, c)

    pool_off = (0, 64, 96)
    for li in (3, 2, 1, 0):
        c, n, base, pos = level_peers(li)
        for j in range(c):
            if li < 3:
                src = pool.at[pl.ds(pool_off[li], n)]
                row = pl.multiple_of(NEAR + 128 * (li + 1) + core * 64 + pos * n, 16)
                dst_ref = kall.at[pl.ds(row, n)]
            else:
                src = pool5
                dst_ref = buf5.at[core * 8 + pos]
            remote(src, dst_ref, pool_send.at[li], pool_recv.at[li], (base + j) * 2 + across, z).start()

    own = kall.at[pl.ds(TOK, TOK)]
    near_p = remote(
        own, kall.at[pl.ds(pl.multiple_of(core * 512, 256), TOK)],
        near_send.at[0], near_recv.at[0], partner, z,
    )
    near_o = remote(
        own, kall.at[pl.ds(pl.multiple_of((1 - core) * 512, 256), TOK)],
        near_send.at[1], near_recv.at[1], other, z,
    )
    near_p.start()
    near_o.start()

    qb = lax.div(iota((128, TOK), 1), 128) + 2 * d
    r = iota((128, TOK), 0)
    kb = 2 * partner + (r >> 6)
    cbias[0:128] = jnp.where(jnp.abs(kb - qb) > 2, 1.0, NEG_BIG)
    for li in range(4):
        c, n, base, pos = level_peers(li)
        rr = r & 63
        chips = base + (rr >> (6 - li))
        first = (chips * 2 + (r >> 6)) * TOK + (rr & (n - 1)) * (4 << li)
        cbias[128 * (li + 1) : 128 * (li + 2)] = jnp.where(
            jnp.abs((first >> 7) - qb) > 2, float(li + 2), NEG_BIG
        )
    loads[3].wait()
    loads[4].wait()
    gain = gain_v[...].reshape(1, 256)
    back[...] = (cotv[...].astype(F32) * gain).T
    for load in loads[5:]:
        load.wait()
    loads[2].wait()

    def half_ref(li, which):
        if li < 3:
            row = pl.multiple_of(NEAR + 128 * (li + 1) + which * 64, 64)
            return kall.at[pl.ds(row, 64)]
        return buf5.at[pl.ds(which * 8, 8)]

    def kcols(h):
        return slice(h * HS, (h + 1) * HS)

    def vcols(h):
        return slice(256 + h * HS, 256 + (h + 1) * HS)

    def group(h, lo, hi, bias):
        s = dot(kall[lo:hi, kcols(h)], qv[:, kcols(h)], 1, 1) * (SCALE * LOG2E) + bias
        top = jnp.max(s, axis=0, keepdims=True)
        p = jnp.exp2(s - top)
        total = jnp.sum(p, axis=0, keepdims=True)
        pt[h, lo:hi, :] = p.astype(BF16)
        out = dot(kall[lo:hi, vcols(h)], pt[h, lo:hi, :], 0, 0)
        return top, total, out

    lane_block = lax.div(iota((1, TOK), 1), 128)
    rows_bias = []
    for e in range(6):
        vals = []
        for i in range(2):
            if e - i < 0 or e - i > 4:
                vals.append(NEG_BIG)
                continue
            want = 2 * d - 2 + e
            hit = jnp.int32(0)
            for j in range(SLOTS):
                ok = jnp.where(nb_ref[i, j] == want, 1, 0) * jnp.where(nc_ref[i] > j, 1, 0)
                hit = jnp.maximum(hit, ok)
            vals.append(jnp.where(hit > 0, 0.0, NEG_BIG))
        row = jnp.where(lane_block == 0, vals[0], vals[1])
        rows_bias.append(jnp.broadcast_to(row, (128, TOK)))
    nbias = jnp.concatenate(rows_bias, axis=0)
    fwds = [None] * 4

    def relay(li):
        mine = half_ref(li, across)
        wait_bytes(mine, pool_recv.at[li])
        fwds[li] = remote(mine, mine, fwd_send.at[li], fwd_recv.at[li], partner, z)
        fwds[li].start()

    for li in range(4):
        relay(li)
    near_p.wait_recv()

    p1 = pool_matrix(128, 1).astype(BF16)
    part = kall[pl.ds(pl.multiple_of((1 - core) * 512, 256), TOK), :]
    kall[NEAR : NEAR + 128, :] = dot(p1, part, 1, 0).astype(BF16)

    for li in range(4):
        fwds[li].wait_recv()
    five = buf5[...].astype(F32)
    kall[ROWS - 128 : ROWS, 0:256] = five[:, 0:8, :].reshape(128, 256).astype(BF16)
    kall[ROWS - 128 : ROWS, 256:512] = five[:, 8:16, :].reshape(128, 256).astype(BF16)

    coarse = [group(h, NEAR, ROWS, cbias[...]) for h in range(2)]
    near_o.wait_recv()
    near = [group(h, 0, NEAR, nbias) for h in range(2)]

    attn, alphas, scaled = [], [], []
    usum = jnp.zeros((1, TOK), F32)
    vsum = jnp.zeros((1, TOK), F32)
    for h in range(2):
        m1, t1, o1 = near[h]
        m2, t2, o2 = coarse[h]
        top = jnp.maximum(m1, m2)
        a1 = jnp.exp2(m1 - top)
        a2 = jnp.exp2(m2 - top)
        inv_total = 1.0 / (a1 * t1 + a2 * t2)
        a1 = a1 * inv_total
        a2 = a2 * inv_total
        out = o1 * a1 + o2 * a2
        sc = out * hs_ref[h]
        usum = usum + jnp.sum(sc * sc, axis=0, keepdims=True)
        vsum = vsum + jnp.sum(sc * back[kcols(h), :], axis=0, keepdims=True)
        attn.append(out)
        alphas.append((a1, a2))
        scaled.append(sc)
    ps_own[0:1, :] = usum
    ps_own[1:2, :] = vsum
    for m in range(1, n_head):
        remote(
            ps_own, ps_buf.at[m - 1], ps_sem.at[0], ps_sem.at[1], d, lax.rem(z + m, n_head)
        ).start()

    u = iota((TOK, TOK), 0)
    col = iota((TOK, TOK), 1)
    lvl = (col >> 6) + 2
    rel = (col & 63) & ((256 >> lvl) - 1)
    spread = jnp.where(
        (u >> lvl) == rel,
        jnp.where(lvl == 2, 0.25, jnp.where(lvl == 3, 0.125, jnp.where(lvl == 4, 0.0625, 0.03125))),
        0.0,
    ).astype(BF16)
    e1 = jnp.where(
        (iota((TOK, 128), 0) >> 1) == iota((TOK, 128), 1), 0.5, 0.0
    ).astype(BF16)

    wait_bytes(ps_buf, ps_sem.at[1])
    sums = ps_own[...] + jnp.sum(ps_buf[...], axis=0)
    inv = lax.rsqrt(sums[0:1, :] / width + NORM_EPS)
    fac = inv * inv * (sums[1:2, :] / width)

    d_group = []
    for h in range(2):
        d_attn = (inv * hs_ref[h]) * (back[kcols(h), :] - scaled[h] * fac)
        d_group.append([(d_attn * a).astype(BF16) for a in alphas[h]])

    def backward(h, g, lo, hi, keep, off):
        dg = d_group[h][g]
        delta = jnp.sum(dg.astype(F32) * attn[h], axis=0, keepdims=True)
        dp = dot(kall[lo:hi, vcols(h)], dg, 1, 0)
        pg = pt[h, lo:hi, :]
        ds = (pg.astype(F32) * (dp - delta)).astype(BF16)
        dst[h, lo:hi, :] = ds
        keep[:, kcols(h)] = dot(ds, qv[:, kcols(h)], 1, 0) * SCALE
        keep[:, vcols(h)] = dot(pg, dg, 1, 1)

    for h in range(2):
        backward(h, 1, NEAR, ROWS, cg, NEAR)
    for li in range(4):
        row = pl.multiple_of(128 * (li + 1) + core * 64, 64)
        c_send[64 * li : 64 * (li + 1), :] = cg[pl.ds(row, 64), :].astype(BF16)
    swap = remote(c_send, c_recv, cp_sem.at[0], cp_sem.at[1], partner, z)
    swap.start()

    for h in range(2):
        backward(h, 0, 0, NEAR, ext, 0)
    rim_out[1] = ext[pl.ds(pl.multiple_of(core * 512, 256), TOK), :].astype(BF16)
    rim_o = remote(rim_out.at[1], rim_in.at[1], rim_send.at[1], rim_recv.at[1], other, z)
    rim_o.start()
    rim_out[0] = (
        ext[pl.ds(pl.multiple_of((1 - core) * 512, 256), TOK), :]
        + dot(e1, cg[0:128, :].astype(BF16), 1, 0)
    ).astype(BF16)
    rim_p = remote(rim_out.at[0], rim_in.at[0], rim_send.at[0], rim_recv.at[0], partner, z)
    rim_p.start()

    swap.wait_recv()
    for li in (3, 2, 1, 0):
        row = pl.multiple_of(128 * (li + 1) + across * 64, 64)
        total = cg[pl.ds(row, 64), :] + c_recv[64 * li : 64 * (li + 1), :].astype(F32)
        if li < 3:
            csum[64 * li : 64 * (li + 1), :] = total.astype(BF16)
        else:
            csum5[...] = jnp.concatenate(
                [total[:, 0:256].reshape(8, 8, 256), total[:, 256:512].reshape(8, 8, 256)], axis=1
            ).astype(BF16)
        c, n, base, pos = level_peers(li)
        for j in range(c):
            if li < 3:
                src = csum.at[pl.ds(64 * li + j * n, n)]
                dst_ref = ret.at[pl.ds(pl.multiple_of(64 * li + pos * n, 16), n)]
            else:
                src = csum5.at[j]
                dst_ref = ret5.at[pos]
            remote(src, dst_ref, ret_send.at[li], ret_recv.at[li], (base + j) * 2 + across, z).start()

    for h in range(2):
        mixed_v[:, kcols(h)] = ((scaled[h] * inv).T * gain[:, kcols(h)]).astype(BF16)
    for h in range(2):
        gqt = dot(kall[:, kcols(h)], dst[h], 0, 0) * SCALE
        gq_v[:, kcols(h)] = gqt.T.astype(BF16)

    rim_p.wait_recv()
    rim_o.wait_recv()
    grad = ext[TOK : 2 * TOK, :] + rim_in[0].astype(F32) + rim_in[1].astype(F32)
    for li in range(3):
        wait_bytes(ret.at[pl.ds(64 * li, 64)], ret_recv.at[li])
    wait_bytes(ret5, ret_recv.at[3])
    last = ret5[...].astype(F32)
    last = jnp.concatenate(
        [last[:, 0:8, :].reshape(64, 256), last[:, 8:16, :].reshape(64, 256)], axis=1
    ).astype(BF16)
    whole = jnp.concatenate([ret[...], last], axis=0)
    grad = grad + dot(spread, whole, 1, 0)
    gk_v[...] = grad[:, 0:256].astype(BF16)
    gv_v[...] = grad[:, 256:512].astype(BF16)

    for li in range(4):
        shape = ret.at[pl.ds(64 * min(li, 2), 64)] if li < 3 else ret5
        wait_bytes(shape, pool_send.at[li])
        wait_bytes(shape, ret_send.at[li])
        fwds[li].wait_send()
    near_p.wait_send()
    near_o.wait_send()
    wait_bytes(ps_buf, ps_sem.at[0])
    swap.wait_send()
    rim_p.wait_send()
    rim_o.wait_send()


def store(a, b, c, e, a_hbm, b_hbm, c_hbm, e_hbm, sem):
    copies = [
        pltpu.make_async_copy(src, dst_ref, sem.at[i])
        for i, (src, dst_ref) in enumerate(((a, a_hbm), (b, b_hbm), (c, c_hbm), (e, e_hbm)))
    ]
    for copy in copies:
        copy.start()
    for copy in copies:
        copy.wait()


def solution(mesh):
    n_ctx, n_head = mesh.shape["ctx"], mesh.shape["head"]
    hbm = pl.BlockSpec(memory_space=pl.ANY)
    vmem = pl.BlockSpec(memory_space=pltpu.VMEM)
    dma = pltpu.SemaphoreType.DMA

    def body(queries, keys, values, near_blocks, near_count, head_scale, gain, cotangent):
        out = jax.ShapeDtypeStruct((TOK, 256), BF16)
        outs = pl.pallas_call(
            functools.partial(kernel, n_ctx, n_head),
            out_shape=(pltpu.VMEM((TOK, 256), BF16),) * 4,
            in_specs=[hbm] * 8,
            out_specs=(vmem, vmem, vmem, vmem),
            scratch_shapes=[
                pltpu.SMEM((2, SLOTS), jnp.int32),
                pltpu.SMEM((2,), jnp.int32),
                pltpu.SMEM((2,), F32),
                pltpu.VMEM((256,), F32),
                pltpu.VMEM((ROWS, COLS), BF16),
                pltpu.VMEM((TOK, 256), BF16),
                pltpu.VMEM((TOK, 256), BF16),
                pltpu.VMEM((112, COLS), BF16),
                pltpu.VMEM((16, 256), BF16),
                pltpu.VMEM((16, 16, 256), BF16),
                pltpu.VMEM((2, TOK), F32),
                pltpu.VMEM((n_head - 1, 2, TOK), F32),
                pltpu.VMEM((COARSE, TOK), F32),
                pltpu.VMEM((256, TOK), F32),
                pltpu.VMEM((2, ROWS, TOK), BF16),
                pltpu.VMEM((2, ROWS, TOK), BF16),
                pltpu.VMEM((COARSE, COLS), F32),
                pltpu.VMEM((NEAR, COLS), F32),
                pltpu.VMEM((256, COLS), BF16),
                pltpu.VMEM((256, COLS), BF16),
                pltpu.VMEM((2, TOK, COLS), BF16),
                pltpu.VMEM((2, TOK, COLS), BF16),
                pltpu.VMEM((192, COLS), BF16),
                pltpu.VMEM((8, 16, 256), BF16),
                pltpu.VMEM((192, COLS), BF16),
                pltpu.VMEM((8, 16, 256), BF16),
                dma((8,)), dma((4,)), dma((4,)), dma((4,)), dma((4,)),
                dma((2,)), dma((2,)), dma((2,)), dma((2,)), dma((2,)), dma((2,)),
                dma((4,)), dma((4,)),
            ],
            compiler_params=pltpu.CompilerParams(
                collective_id=0, has_side_effects=True, vmem_limit_bytes=56 * 1024 * 1024
            ),
        )(queries, keys, values, near_blocks, near_count, head_scale, gain, cotangent)
        return pl.pallas_call(
            store,
            out_shape=(out, out, out, out),
            in_specs=[hbm] * 4,
            out_specs=(hbm, hbm, hbm, hbm),
            scratch_shapes=[dma((4,))],
            compiler_params=pltpu.CompilerParams(vmem_limit_bytes=1024 * 1024),
        )(*outs)

    return jax.shard_map(
        body,
        mesh=mesh,
        in_specs=(
            P("ctx", "head"), P("ctx", "head"), P("ctx", "head"), P("ctx", None),
            P("ctx"), P("head"), P("head"), P("ctx", "head"),
        ),
        out_specs=(P("ctx", "head"), P("ctx", "head"), P("ctx", "head"), P("ctx", "head")),
        check_vma=False,
    )
```

```python
import functools
import math

import jax
import jax.numpy as jnp
from jax import lax
from jax.experimental import pallas as pl
from jax.experimental.pallas import tpu as pltpu
from jax.sharding import PartitionSpec as P

HS = 128
BT = 128
SLOTS = 4
NEG_BIG = -1e30
NORM_EPS = 1e-05
LOG2E = 1.4426950408889634
SCALE = 1.0 / math.sqrt(HS)
TOK = 256
COLS = 512
NEAR = 768
ROWS = 1408
COARSE = ROWS - NEAR
F32 = jnp.float32
BF16 = jnp.bfloat16


def dot(a, b, ca, cb):
    return lax.dot_general(
        a, b, (((ca,), (cb,)), ((), ())), preferred_element_type=F32
    )


def iota(shape, dim):
    return lax.broadcasted_iota(jnp.int32, shape, dim)


def pool_matrix(rows, level):
    hit = (iota((rows, TOK), 1) >> level) == iota((rows, TOK), 0)
    return jnp.where(hit, 2.0**-level, 0.0)


def kernel(
    n_ctx, n_head,
    q_hbm, k_hbm, v_hbm, nb_hbm, nc_hbm, hs_hbm, gain_hbm, cot_hbm,
    mixed_v, gq_v, gk_v, gv_v,
    nb_ref, nc_ref, hs_ref, gain_v,
    kall, qv, cotv, pool, pool5, buf5, ps_own, ps_buf, cbias, back,
    pt, dst, cg, ext, c_send, c_recv, rim_out, rim_in, csum, csum5, ret, ret5, ext_o,
    ld_sem, pool_send, pool_recv, fwd_send, fwd_recv, near_send, near_recv,
    ps_sem, cp_sem, rim_send, rim_recv, ret_send, ret_recv,
):
    d = lax.axis_index("ctx")
    z = lax.axis_index("head")
    n_chip = n_ctx // 2
    chip = lax.div(d, 2)
    core = lax.rem(d, 2)
    across = 1 - core
    partner = chip * 2 + across
    other = lax.rem(d + n_ctx - 1 + 2 * core, n_ctx)
    width = float(n_head * 2 * HS)

    barrier = pltpu.get_barrier_semaphore()

    def hello(ctx, head):
        pl.semaphore_signal(
            barrier, inc=1, device_id=(ctx, head), device_id_type=pl.DeviceIdType.MESH
        )

    def remote(src, dst_ref, ssem, rsem, ctx, head):
        return pltpu.make_async_remote_copy(
            src_ref=src, dst_ref=dst_ref, send_sem=ssem, recv_sem=rsem,
            device_id=(ctx, head), device_id_type=pl.DeviceIdType.MESH,
        )

    def wait_bytes(ref, sem):
        pltpu.make_async_copy(ref, ref, sem).wait()

    loads = [
        pltpu.make_async_copy(k_hbm, kall.at[pl.ds(TOK, TOK), pl.ds(0, 256)], ld_sem.at[0]),
        pltpu.make_async_copy(v_hbm, kall.at[pl.ds(TOK, TOK), pl.ds(256, 256)], ld_sem.at[1]),
        pltpu.make_async_copy(q_hbm, qv, ld_sem.at[2]),
        pltpu.make_async_copy(cot_hbm, cotv, ld_sem.at[3]),
        pltpu.make_async_copy(gain_hbm, gain_v, ld_sem.at[4]),
        pltpu.make_async_copy(nb_hbm, nb_ref, ld_sem.at[5]),
        pltpu.make_async_copy(nc_hbm, nc_ref, ld_sem.at[6]),
        pltpu.make_async_copy(hs_hbm, hs_ref, ld_sem.at[7]),
    ]
    for load in loads:
        load.start()
    for m in range(1, n_chip):
        hello(lax.rem(chip + m, n_chip) * 2 + across, z)
    hello(partner, z)
    for m in range(1, n_head):
        hello(d, lax.rem(z + m, n_head))

    pm = jnp.concatenate(
        [pool_matrix(64, 2), pool_matrix(32, 3), pool_matrix(16, 4), pool_matrix(8, 5),
         jnp.zeros((8, TOK), F32)], axis=0,
    ).astype(BF16)
    loads[0].wait()
    loads[1].wait()
    pooled = dot(pm, kall[TOK : 2 * TOK, :], 1, 0)
    pool[...] = pooled[0:112].astype(BF16)
    pool5[...] = jnp.concatenate([pooled[112:120, 0:256], pooled[112:120, 256:512]], axis=0).astype(BF16)

    pl.semaphore_wait(barrier, n_head - 1 + n_chip - 1 + 1)

    def level_peers(li):
        c = 1 << li
        half = lax.div(chip, c)
        base = (half + 1 - 2 * lax.rem(half, 2)) * c
        return c, 64 >> li, base, lax.rem(chip, c)

    pool_off = (0, 64, 96)
    for li in (3, 2, 1, 0):
        c, n, base, pos = level_peers(li)
        for j in range(c):
            if li < 3:
                src = pool.at[pl.ds(pool_off[li], n)]
                row = pl.multiple_of(NEAR + 128 * (li + 1) + core * 64 + pos * n, 16)
                dst_ref = kall.at[pl.ds(row, n)]
            else:
                src = pool5
                dst_ref = buf5.at[core * 8 + pos]
            remote(src, dst_ref, pool_send.at[li], pool_recv.at[li], (base + j) * 2 + across, z).start()

    own = kall.at[pl.ds(TOK, TOK)]
    near_p = remote(
        own, kall.at[pl.ds(pl.multiple_of(core * 512, 256), TOK)],
        near_send.at[0], near_recv.at[0], partner, z,
    )
    near_o = remote(
        own, kall.at[pl.ds(pl.multiple_of((1 - core) * 512, 256), TOK)],
        near_send.at[1], near_recv.at[1], other, z,
    )
    near_p.start()
    near_o.start()

    qb = lax.div(iota((128, TOK), 1), 128) + 2 * d
    r = iota((128, TOK), 0)
    kb = 2 * partner + (r >> 6)
    cbias[0:128] = jnp.where(jnp.abs(kb - qb) > 2, 1.0, NEG_BIG)
    for li in range(4):
        c, n, base, pos = level_peers(li)
        rr = r & 63
        chips = base + (rr >> (6 - li))
        first = (chips * 2 + (r >> 6)) * TOK + (rr & (n - 1)) * (4 << li)
        cbias[128 * (li + 1) : 128 * (li + 2)] = jnp.where(
            jnp.abs((first >> 7) - qb) > 2, float(li + 2), NEG_BIG
        )
    loads[3].wait()
    loads[4].wait()
    gain = gain_v[...].reshape(1, 256)
    back[...] = (cotv[...].astype(F32) * gain).T
    for load in loads[5:]:
        load.wait()
    loads[2].wait()

    def half_ref(li, which):
        if li < 3:
            row = pl.multiple_of(NEAR + 128 * (li + 1) + which * 64, 64)
            return kall.at[pl.ds(row, 64)]
        return buf5.at[pl.ds(which * 8, 8)]

    def kcols(h):
        return slice(h * HS, (h + 1) * HS)

    def vcols(h):
        return slice(256 + h * HS, 256 + (h + 1) * HS)

    local = pl.ds(pl.multiple_of(across * 256, 256), 512)
    beside = pl.ds(pl.multiple_of(core * 512, 256), 256)
    far = pl.ds(NEAR, COARSE)

    def group(h, rows, bias):
        s = dot(kall[rows, kcols(h)], qv[:, kcols(h)], 1, 1) * (SCALE * LOG2E) + bias
        top = jnp.max(s, axis=0, keepdims=True)
        p = jnp.exp2(s - top)
        total = jnp.sum(p, axis=0, keepdims=True)
        pb = p.astype(BF16)
        pt[h, rows, :] = pb
        out = dot(kall[rows, vcols(h)], pb, 0, 0)
        return top, total, out

    lane_block = lax.div(iota((1, TOK), 1), 128)

    def list_bias(first, count):
        rows_bias = []
        for e in range(count):
            vals = []
            for i in range(2):
                hit = jnp.int32(0)
                for j in range(SLOTS):
                    ok = jnp.where(nb_ref[i, j] == first + e, 1, 0) * jnp.where(nc_ref[i] > j, 1, 0)
                    hit = jnp.maximum(hit, ok)
                vals.append(jnp.where(hit > 0, 0.0, NEG_BIG))
            row = jnp.where(lane_block == 0, vals[0], vals[1])
            rows_bias.append(jnp.broadcast_to(row, (128, TOK)))
        return jnp.concatenate(rows_bias, axis=0)

    near_p.wait_recv()
    local_bias = list_bias(2 * d - 2 + 2 * across, 4)
    inner = [group(h, local, local_bias) for h in range(2)]

    p1 = pool_matrix(128, 1).astype(BF16)
    part = kall[pl.ds(pl.multiple_of(across * 512, 256), TOK), :]
    kall[NEAR : NEAR + 128, :] = dot(p1, part, 1, 0).astype(BF16)

    fwds = [None] * 4

    def relay(li):
        mine = half_ref(li, across)
        wait_bytes(mine, pool_recv.at[li])
        fwds[li] = remote(mine, mine, fwd_send.at[li], fwd_recv.at[li], partner, z)
        fwds[li].start()

    for li in range(4):
        relay(li)
    for li in range(4):
        fwds[li].wait_recv()
    five = buf5[...].astype(F32)
    kall[ROWS - 128 : ROWS, 0:256] = five[:, 0:8, :].reshape(128, 256).astype(BF16)
    kall[ROWS - 128 : ROWS, 256:512] = five[:, 8:16, :].reshape(128, 256).astype(BF16)

    coarse = [group(h, far, cbias[...]) for h in range(2)]

    near_o.wait_recv()
    beside_bias = list_bias(2 * d - 2 + 4 * core, 2)
    outer = [group(h, beside, beside_bias) for h in range(2)]

    attn, alphas, scaled = [], [], []
    usum = jnp.zeros((1, TOK), F32)
    vsum = jnp.zeros((1, TOK), F32)
    for h in range(2):
        parts = (coarse[h], inner[h], outer[h])
        top = functools.reduce(jnp.maximum, [part[0] for part in parts])
        factors = [jnp.exp2(part[0] - top) for part in parts]
        inv_total = 1.0 / sum(f * part[1] for f, part in zip(factors, parts))
        factors = [f * inv_total for f in factors]
        out = sum(f * part[2] for f, part in zip(factors, parts))
        sc = out * hs_ref[h]
        usum = usum + jnp.sum(sc * sc, axis=0, keepdims=True)
        vsum = vsum + jnp.sum(sc * back[kcols(h), :], axis=0, keepdims=True)
        attn.append(out)
        alphas.append(factors)
        scaled.append(sc)
    ps_own[0:1, :] = usum
    ps_own[1:2, :] = vsum
    for m in range(1, n_head):
        remote(
            ps_own, ps_buf.at[m - 1], ps_sem.at[0], ps_sem.at[1], d, lax.rem(z + m, n_head)
        ).start()

    u = iota((TOK, TOK), 0)
    col = iota((TOK, TOK), 1)
    lvl = (col >> 6) + 2
    rel = (col & 63) & ((256 >> lvl) - 1)
    spread = jnp.where(
        (u >> lvl) == rel,
        jnp.where(lvl == 2, 0.25, jnp.where(lvl == 3, 0.125, jnp.where(lvl == 4, 0.0625, 0.03125))),
        0.0,
    ).astype(BF16)
    e1 = jnp.where(
        (iota((TOK, 128), 0) >> 1) == iota((TOK, 128), 1), 0.5, 0.0
    ).astype(BF16)

    wait_bytes(ps_buf, ps_sem.at[1])
    sums = ps_own[...] + jnp.sum(ps_buf[...], axis=0)
    inv = lax.rsqrt(sums[0:1, :] / width + NORM_EPS)
    fac = inv * inv * (sums[1:2, :] / width)

    d_group = []
    for h in range(2):
        d_attn = (inv * hs_ref[h]) * (back[kcols(h), :] - scaled[h] * fac)
        d_group.append([(d_attn * a).astype(BF16) for a in alphas[h]])

    def backward(h, g, rows, keep):
        dg = d_group[h][g]
        delta = jnp.sum(dg.astype(F32) * attn[h], axis=0, keepdims=True)
        dp = dot(kall[rows, vcols(h)], dg, 1, 0)
        pg = pt[h, rows, :]
        ds = (pg.astype(F32) * (dp - delta)).astype(BF16)
        dst[h, rows, :] = ds
        keep[:, kcols(h)] = dot(ds, qv[:, kcols(h)], 1, 0) * SCALE
        keep[:, vcols(h)] = dot(pg, dg, 1, 1)

    for h in range(2):
        backward(h, 0, far, cg)
    for li in range(4):
        row = pl.multiple_of(128 * (li + 1) + core * 64, 64)
        c_send[64 * li : 64 * (li + 1), :] = cg[pl.ds(row, 64), :].astype(BF16)
    swap = remote(c_send, c_recv, cp_sem.at[0], cp_sem.at[1], partner, z)
    swap.start()

    for h in range(2):
        backward(h, 2, beside, ext_o)
    rim_out[1] = ext_o[...].astype(BF16)
    rim_o = remote(rim_out.at[1], rim_in.at[1], rim_send.at[1], rim_recv.at[1], other, z)
    rim_o.start()
    backward(0, 1, local, ext)

    swap.wait_recv()
    for li in (3, 2, 1, 0):
        row = pl.multiple_of(128 * (li + 1) + across * 64, 64)
        total = cg[pl.ds(row, 64), :] + c_recv[64 * li : 64 * (li + 1), :].astype(F32)
        if li < 3:
            csum[64 * li : 64 * (li + 1), :] = total.astype(BF16)
        else:
            csum5[...] = jnp.concatenate(
                [total[:, 0:256].reshape(8, 8, 256), total[:, 256:512].reshape(8, 8, 256)], axis=1
            ).astype(BF16)
        c, n, base, pos = level_peers(li)
        for j in range(c):
            if li < 3:
                src = csum.at[pl.ds(64 * li + j * n, n)]
                dst_ref = ret.at[pl.ds(pl.multiple_of(64 * li + pos * n, 16), n)]
            else:
                src = csum5.at[j]
                dst_ref = ret5.at[pos]
            remote(src, dst_ref, ret_send.at[li], ret_recv.at[li], (base + j) * 2 + across, z).start()

    backward(1, 1, local, ext)
    rim_out[0] = (
        ext[pl.ds(pl.multiple_of(across * 256, 256), TOK), :]
        + dot(e1, cg[0:128, :].astype(BF16), 1, 0)
    ).astype(BF16)
    rim_p = remote(rim_out.at[0], rim_in.at[0], rim_send.at[0], rim_recv.at[0], partner, z)
    rim_p.start()

    for h in range(2):
        mixed_v[:, kcols(h)] = ((scaled[h] * inv).T * gain[:, kcols(h)]).astype(BF16)
    for h in range(2):
        gqt = dot(kall[:, kcols(h)], dst[h], 0, 0) * SCALE
        gq_v[:, kcols(h)] = gqt.T.astype(BF16)

    rim_p.wait_recv()
    rim_o.wait_recv()
    grad = ext[pl.ds(pl.multiple_of(core * 256, 256), TOK), :] + rim_in[0].astype(F32) + rim_in[1].astype(F32)
    for li in range(3):
        wait_bytes(ret.at[pl.ds(64 * li, 64)], ret_recv.at[li])
    wait_bytes(ret5, ret_recv.at[3])
    last = ret5[...].astype(F32)
    last = jnp.concatenate(
        [last[:, 0:8, :].reshape(64, 256), last[:, 8:16, :].reshape(64, 256)], axis=1
    ).astype(BF16)
    whole = jnp.concatenate([ret[...], last], axis=0)
    grad = grad + dot(spread, whole, 1, 0)
    gk_v[...] = grad[:, 0:256].astype(BF16)
    gv_v[...] = grad[:, 256:512].astype(BF16)

    for li in range(4):
        shape = ret.at[pl.ds(64 * min(li, 2), 64)] if li < 3 else ret5
        wait_bytes(shape, pool_send.at[li])
        wait_bytes(shape, ret_send.at[li])
        fwds[li].wait_send()
    near_p.wait_send()
    near_o.wait_send()
    wait_bytes(ps_buf, ps_sem.at[0])
    swap.wait_send()
    rim_p.wait_send()
    rim_o.wait_send()


def store(a, b, c, e, a_hbm, b_hbm, c_hbm, e_hbm, sem):
    copies = [
        pltpu.make_async_copy(src, dst_ref, sem.at[i])
        for i, (src, dst_ref) in enumerate(((a, a_hbm), (b, b_hbm), (c, c_hbm), (e, e_hbm)))
    ]
    for copy in copies:
        copy.start()
    for copy in copies:
        copy.wait()


def solution(mesh):
    n_ctx, n_head = mesh.shape["ctx"], mesh.shape["head"]
    hbm = pl.BlockSpec(memory_space=pl.ANY)
    vmem = pl.BlockSpec(memory_space=pltpu.VMEM)
    dma = pltpu.SemaphoreType.DMA

    def body(queries, keys, values, near_blocks, near_count, head_scale, gain, cotangent):
        out = jax.ShapeDtypeStruct((TOK, 256), BF16)
        outs = pl.pallas_call(
            functools.partial(kernel, n_ctx, n_head),
            out_shape=(pltpu.VMEM((TOK, 256), BF16),) * 4,
            in_specs=[hbm] * 8,
            out_specs=(vmem, vmem, vmem, vmem),
            scratch_shapes=[
                pltpu.SMEM((2, SLOTS), jnp.int32),
                pltpu.SMEM((2,), jnp.int32),
                pltpu.SMEM((2,), F32),
                pltpu.VMEM((256,), F32),
                pltpu.VMEM((ROWS, COLS), BF16),
                pltpu.VMEM((TOK, 256), BF16),
                pltpu.VMEM((TOK, 256), BF16),
                pltpu.VMEM((112, COLS), BF16),
                pltpu.VMEM((16, 256), BF16),
                pltpu.VMEM((16, 16, 256), BF16),
                pltpu.VMEM((2, TOK), F32),
                pltpu.VMEM((n_head - 1, 2, TOK), F32),
                pltpu.VMEM((COARSE, TOK), F32),
                pltpu.VMEM((256, TOK), F32),
                pltpu.VMEM((2, ROWS, TOK), BF16),
                pltpu.VMEM((2, ROWS, TOK), BF16),
                pltpu.VMEM((COARSE, COLS), F32),
                pltpu.VMEM((512, COLS), F32),
                pltpu.VMEM((256, COLS), BF16),
                pltpu.VMEM((256, COLS), BF16),
                pltpu.VMEM((2, TOK, COLS), BF16),
                pltpu.VMEM((2, TOK, COLS), BF16),
                pltpu.VMEM((192, COLS), BF16),
                pltpu.VMEM((8, 16, 256), BF16),
                pltpu.VMEM((192, COLS), BF16),
                pltpu.VMEM((8, 16, 256), BF16),
                pltpu.VMEM((TOK, COLS), F32),
                dma((8,)), dma((4,)), dma((4,)), dma((4,)), dma((4,)),
                dma((2,)), dma((2,)), dma((2,)), dma((2,)), dma((2,)), dma((2,)),
                dma((4,)), dma((4,)),
            ],
            compiler_params=pltpu.CompilerParams(
                collective_id=0, has_side_effects=True, vmem_limit_bytes=56 * 1024 * 1024
            ),
        )(queries, keys, values, near_blocks, near_count, head_scale, gain, cotangent)
        return pl.pallas_call(
            store,
            out_shape=(out, out, out, out),
            in_specs=[hbm] * 4,
            out_specs=(hbm, hbm, hbm, hbm),
            scratch_shapes=[dma((4,))],
            compiler_params=pltpu.CompilerParams(vmem_limit_bytes=1024 * 1024),
        )(*outs)

    return jax.shard_map(
        body,
        mesh=mesh,
        in_specs=(
            P("ctx", "head"), P("ctx", "head"), P("ctx", "head"), P("ctx", None),
            P("ctx"), P("head"), P("head"), P("ctx", "head"),
        ),
        out_specs=(P("ctx", "head"), P("ctx", "head"), P("ctx", "head"), P("ctx", "head")),
        check_vma=False,
    )
```

```python
import functools
import math

import jax
import jax.numpy as jnp
from jax import lax
from jax.experimental import pallas as pl
from jax.experimental.pallas import tpu as pltpu
from jax.sharding import PartitionSpec as P

HS = 128
BT = 128
SLOTS = 4
NEG_BIG = -1e30
NORM_EPS = 1e-05
LOG2E = 1.4426950408889634
SCALE = 1.0 / math.sqrt(HS)
TOK = 256
COLS = 512
NEAR = 768
ROWS = 1408
COARSE = ROWS - NEAR
F32 = jnp.float32
BF16 = jnp.bfloat16


def dot(a, b, ca, cb):
    return lax.dot_general(
        a, b, (((ca,), (cb,)), ((), ())), preferred_element_type=F32
    )


def iota(shape, dim):
    return lax.broadcasted_iota(jnp.int32, shape, dim)


def pool_matrix(rows, level):
    hit = (iota((rows, TOK), 1) >> level) == iota((rows, TOK), 0)
    return jnp.where(hit, 2.0**-level, 0.0)


def kernel(
    n_ctx, n_head,
    q_hbm, k_hbm, v_hbm, nb_hbm, nc_hbm, hs_hbm, gain_hbm, cot_hbm,
    mixed_v, gq_v, gk_v, gv_v,
    nb_ref, nc_ref, hs_ref, gain_v,
    kall, qv, cotv, pool, pool5, buf5, ps_own, ps_buf, cbias, back,
    pt, dst, cg, ext, c_send, c_recv, rim_out, rim_in, csum, csum5, ret, ret5, ext_o,
    ld_sem, pool_send, pool_recv, fwd_send, fwd_recv, near_send, near_recv,
    ps_sem, cp_sem, rim_send, rim_recv, ret_send, ret_recv,
):
    d = lax.axis_index("ctx")
    z = lax.axis_index("head")
    n_chip = n_ctx // 2
    chip = lax.div(d, 2)
    core = lax.rem(d, 2)
    across = 1 - core
    partner = chip * 2 + across
    other = lax.rem(d + n_ctx - 1 + 2 * core, n_ctx)
    width = float(n_head * 2 * HS)

    barrier = pltpu.get_barrier_semaphore()

    def hello(ctx, head):
        pl.semaphore_signal(
            barrier, inc=1, device_id=(ctx, head), device_id_type=pl.DeviceIdType.MESH
        )

    def remote(src, dst_ref, ssem, rsem, ctx, head):
        return pltpu.make_async_remote_copy(
            src_ref=src, dst_ref=dst_ref, send_sem=ssem, recv_sem=rsem,
            device_id=(ctx, head), device_id_type=pl.DeviceIdType.MESH,
        )

    def wait_bytes(ref, sem):
        pltpu.make_async_copy(ref, ref, sem).wait()

    loads = [
        pltpu.make_async_copy(k_hbm, kall.at[pl.ds(TOK, TOK), pl.ds(0, 256)], ld_sem.at[0]),
        pltpu.make_async_copy(v_hbm, kall.at[pl.ds(TOK, TOK), pl.ds(256, 256)], ld_sem.at[1]),
        pltpu.make_async_copy(q_hbm, qv, ld_sem.at[2]),
        pltpu.make_async_copy(cot_hbm, cotv, ld_sem.at[3]),
        pltpu.make_async_copy(gain_hbm, gain_v, ld_sem.at[4]),
        pltpu.make_async_copy(nb_hbm, nb_ref, ld_sem.at[5]),
        pltpu.make_async_copy(nc_hbm, nc_ref, ld_sem.at[6]),
        pltpu.make_async_copy(hs_hbm, hs_ref, ld_sem.at[7]),
    ]
    for load in loads:
        load.start()
    for m in range(1, n_chip):
        hello(lax.rem(chip + m, n_chip) * 2 + across, z)
    hello(partner, z)
    for m in range(1, n_head):
        hello(d, lax.rem(z + m, n_head))

    pm = jnp.concatenate(
        [pool_matrix(64, 2), pool_matrix(32, 3), pool_matrix(16, 4), pool_matrix(8, 5),
         jnp.zeros((8, TOK), F32)], axis=0,
    ).astype(BF16)
    loads[0].wait()
    loads[1].wait()
    pooled = dot(pm, kall[TOK : 2 * TOK, :], 1, 0)
    pool[...] = pooled[0:112].astype(BF16)
    pool5[...] = jnp.concatenate([pooled[112:120, 0:256], pooled[112:120, 256:512]], axis=0).astype(BF16)

    pl.semaphore_wait(barrier, n_head - 1 + n_chip - 1 + 1)

    def level_peers(li):
        c = 1 << li
        half = lax.div(chip, c)
        base = (half + 1 - 2 * lax.rem(half, 2)) * c
        return c, 64 >> li, base, lax.rem(chip, c)

    pool_off = (0, 64, 96)
    for li in (3, 2, 1, 0):
        c, n, base, pos = level_peers(li)
        for j in range(c):
            if li < 3:
                src = pool.at[pl.ds(pool_off[li], n)]
                row = pl.multiple_of(NEAR + 128 * (li + 1) + core * 64 + pos * n, 16)
                dst_ref = kall.at[pl.ds(row, n)]
            else:
                src = pool5
                dst_ref = buf5.at[core * 8 + pos]
            remote(src, dst_ref, pool_send.at[li], pool_recv.at[li], (base + j) * 2 + across, z).start()

    own = kall.at[pl.ds(TOK, TOK)]
    near_p = remote(
        own, kall.at[pl.ds(pl.multiple_of(core * 512, 256), TOK)],
        near_send.at[0], near_recv.at[0], partner, z,
    )
    near_o = remote(
        own, kall.at[pl.ds(pl.multiple_of((1 - core) * 512, 256), TOK)],
        near_send.at[1], near_recv.at[1], other, z,
    )
    near_p.start()
    near_o.start()

    qb = lax.div(iota((128, TOK), 1), 128) + 2 * d
    r = iota((128, TOK), 0)
    kb = 2 * partner + (r >> 6)
    cbias[0:128] = jnp.where(jnp.abs(kb - qb) > 2, 1.0, NEG_BIG)
    for li in range(4):
        c, n, base, pos = level_peers(li)
        rr = r & 63
        chips = base + (rr >> (6 - li))
        first = (chips * 2 + (r >> 6)) * TOK + (rr & (n - 1)) * (4 << li)
        cbias[128 * (li + 1) : 128 * (li + 2)] = jnp.where(
            jnp.abs((first >> 7) - qb) > 2, float(li + 2), NEG_BIG
        )
    loads[3].wait()
    loads[4].wait()
    gain = gain_v[...].reshape(1, 256)
    back[...] = (cotv[...].astype(F32) * gain).T
    for load in loads[5:]:
        load.wait()
    loads[2].wait()

    def half_ref(li, which):
        if li < 3:
            row = pl.multiple_of(NEAR + 128 * (li + 1) + which * 64, 64)
            return kall.at[pl.ds(row, 64)]
        return buf5.at[pl.ds(which * 8, 8)]

    def kcols(h):
        return slice(h * HS, (h + 1) * HS)

    def vcols(h):
        return slice(256 + h * HS, 256 + (h + 1) * HS)

    local = pl.ds(pl.multiple_of(across * 256, 256), 512)
    beside = pl.ds(pl.multiple_of(core * 512, 256), 256)
    far = pl.ds(NEAR, COARSE)

    def group(h, rows, bias):
        s = dot(kall[rows, kcols(h)], qv[:, kcols(h)], 1, 1) * (SCALE * LOG2E) + bias
        top = jnp.max(s, axis=0, keepdims=True)
        p = jnp.exp2(s - top)
        total = jnp.sum(p, axis=0, keepdims=True)
        pb = p.astype(BF16)
        pt[h, rows, :] = pb
        out = dot(kall[rows, vcols(h)], pb, 0, 0)
        return top, total, out

    lane_block = lax.div(iota((1, TOK), 1), 128)

    def list_bias(first, count):
        rows_bias = []
        for e in range(count):
            vals = []
            for i in range(2):
                hit = jnp.int32(0)
                for j in range(SLOTS):
                    ok = jnp.where(nb_ref[i, j] == first + e, 1, 0) * jnp.where(nc_ref[i] > j, 1, 0)
                    hit = jnp.maximum(hit, ok)
                vals.append(jnp.where(hit > 0, 0.0, NEG_BIG))
            row = jnp.where(lane_block == 0, vals[0], vals[1])
            rows_bias.append(jnp.broadcast_to(row, (128, TOK)))
        return jnp.concatenate(rows_bias, axis=0)

    near_p.wait_recv()
    local_bias = list_bias(2 * d - 2 + 2 * across, 4)
    inner = [group(h, local, local_bias) for h in range(2)]

    p1 = pool_matrix(128, 1).astype(BF16)
    part = kall[pl.ds(pl.multiple_of(across * 512, 256), TOK), :]
    kall[NEAR : NEAR + 128, :] = dot(p1, part, 1, 0).astype(BF16)

    fwds = [None] * 4

    def relay(li):
        mine = half_ref(li, across)
        wait_bytes(mine, pool_recv.at[li])
        fwds[li] = remote(mine, mine, fwd_send.at[li], fwd_recv.at[li], partner, z)
        fwds[li].start()

    for li in range(4):
        relay(li)
    for li in range(4):
        fwds[li].wait_recv()
    five = buf5[...].astype(F32)
    kall[ROWS - 128 : ROWS, 0:256] = five[:, 0:8, :].reshape(128, 256).astype(BF16)
    kall[ROWS - 128 : ROWS, 256:512] = five[:, 8:16, :].reshape(128, 256).astype(BF16)

    coarse = [group(h, far, cbias[...]) for h in range(2)]

    near_o.wait_recv()
    beside_bias = list_bias(2 * d - 2 + 4 * core, 2)
    outer = [group(h, beside, beside_bias) for h in range(2)]

    attn, alphas, scaled = [], [], []
    usum = jnp.zeros((1, TOK), F32)
    vsum = jnp.zeros((1, TOK), F32)
    for h in range(2):
        parts = (coarse[h], inner[h], outer[h])
        top = functools.reduce(jnp.maximum, [part[0] for part in parts])
        factors = [jnp.exp2(part[0] - top) for part in parts]
        inv_total = 1.0 / sum(f * part[1] for f, part in zip(factors, parts))
        factors = [f * inv_total for f in factors]
        out = sum(f * part[2] for f, part in zip(factors, parts))
        sc = out * hs_ref[h]
        usum = usum + jnp.sum(sc * sc, axis=0, keepdims=True)
        vsum = vsum + jnp.sum(sc * back[kcols(h), :], axis=0, keepdims=True)
        attn.append(out)
        alphas.append(factors)
        scaled.append(sc)
    ps_own[0:1, :] = usum
    ps_own[1:2, :] = vsum
    for m in sorted(range(1, n_head), key=lambda m: -min(m, n_head - m)):
        remote(
            ps_own, ps_buf.at[m - 1], ps_sem.at[0], ps_sem.at[1], d, lax.rem(z + m, n_head)
        ).start()

    u = iota((TOK, TOK), 0)
    col = iota((TOK, TOK), 1)
    lvl = (col >> 6) + 2
    rel = (col & 63) & ((256 >> lvl) - 1)
    spread = jnp.where(
        (u >> lvl) == rel,
        jnp.where(lvl == 2, 0.25, jnp.where(lvl == 3, 0.125, jnp.where(lvl == 4, 0.0625, 0.03125))),
        0.0,
    ).astype(BF16)
    e1 = jnp.where(
        (iota((TOK, 128), 0) >> 1) == iota((TOK, 128), 1), 0.5, 0.0
    ).astype(BF16)

    wait_bytes(ps_buf, ps_sem.at[1])
    sums = ps_own[...] + jnp.sum(ps_buf[...], axis=0)
    inv = lax.rsqrt(sums[0:1, :] / width + NORM_EPS)
    fac = inv * inv * (sums[1:2, :] / width)

    d_group = []
    for h in range(2):
        d_attn = (inv * hs_ref[h]) * (back[kcols(h), :] - scaled[h] * fac)
        d_group.append([(d_attn * a).astype(BF16) for a in alphas[h]])

    def backward(h, g, rows, keep, to=slice(None)):
        dg = d_group[h][g]
        delta = jnp.sum(dg.astype(F32) * attn[h], axis=0, keepdims=True)
        dp = dot(kall[rows, vcols(h)], dg, 1, 0)
        pg = pt[h, rows, :]
        ds = (pg.astype(F32) * (dp - delta)).astype(BF16)
        dst[h, rows, :] = ds
        keep[to, kcols(h)] = dot(ds, qv[:, kcols(h)], 1, 0) * SCALE
        keep[to, vcols(h)] = dot(pg, dg, 1, 1)

    for h in range(2):
        backward(h, 2, beside, ext_o)
    rim_out[1] = ext_o[...].astype(BF16)
    rim_o = remote(rim_out.at[1], rim_in.at[1], rim_send.at[1], rim_recv.at[1], other, z)
    rim_o.start()
    for h in range(2):
        backward(h, 0, pl.ds(NEAR + 384, 256), cg, slice(384, 640))

    def start_swap(lis, i):
        for li in lis:
            row = pl.multiple_of(128 * (li + 1) + core * 64, 64)
            c_send[64 * li : 64 * (li + 1), :] = cg[pl.ds(row, 64), :].astype(BF16)
        half = pl.ds(64 * lis[0], 128)
        copy = remote(c_send.at[half], c_recv.at[half], cp_sem.at[i], cp_sem.at[2 + i], partner, z)
        copy.start()
        return copy

    swap_far = start_swap((2, 3), 0)
    for h in range(2):
        backward(h, 0, pl.ds(NEAR, 384), cg, slice(0, 384))
    swap = start_swap((0, 1), 1)

    swap_far.wait_recv()
    for li in (3, 2, 1, 0):
        if li == 1:
            backward(0, 1, local, ext)
            swap.wait_recv()
        row = pl.multiple_of(128 * (li + 1) + across * 64, 64)
        total = cg[pl.ds(row, 64), :] + c_recv[64 * li : 64 * (li + 1), :].astype(F32)
        if li < 3:
            csum[64 * li : 64 * (li + 1), :] = total.astype(BF16)
        else:
            csum5[...] = jnp.concatenate(
                [total[:, 0:256].reshape(8, 8, 256), total[:, 256:512].reshape(8, 8, 256)], axis=1
            ).astype(BF16)
        c, n, base, pos = level_peers(li)
        for j in range(c):
            if li < 3:
                src = csum.at[pl.ds(64 * li + j * n, n)]
                dst_ref = ret.at[pl.ds(pl.multiple_of(64 * li + pos * n, 16), n)]
            else:
                src = csum5.at[j]
                dst_ref = ret5.at[pos]
            remote(src, dst_ref, ret_send.at[li], ret_recv.at[li], (base + j) * 2 + across, z).start()

    backward(1, 1, local, ext)
    rim_out[0] = (
        ext[pl.ds(pl.multiple_of(across * 256, 256), TOK), :]
        + dot(e1, cg[0:128, :].astype(BF16), 1, 0)
    ).astype(BF16)
    rim_p = remote(rim_out.at[0], rim_in.at[0], rim_send.at[0], rim_recv.at[0], partner, z)
    rim_p.start()

    for h in range(2):
        mixed_v[:, kcols(h)] = ((scaled[h] * inv).T * gain[:, kcols(h)]).astype(BF16)
    for h in range(2):
        gqt = dot(kall[:, kcols(h)], dst[h], 0, 0) * SCALE
        gq_v[:, kcols(h)] = gqt.T.astype(BF16)

    rim_p.wait_recv()
    rim_o.wait_recv()
    grad = ext[pl.ds(pl.multiple_of(core * 256, 256), TOK), :] + rim_in[0].astype(F32) + rim_in[1].astype(F32)
    for li in range(3):
        wait_bytes(ret.at[pl.ds(64 * li, 64)], ret_recv.at[li])
    wait_bytes(ret5, ret_recv.at[3])
    last = ret5[...].astype(F32)
    last = jnp.concatenate(
        [last[:, 0:8, :].reshape(64, 256), last[:, 8:16, :].reshape(64, 256)], axis=1
    ).astype(BF16)
    whole = jnp.concatenate([ret[...], last], axis=0)
    grad = grad + dot(spread, whole, 1, 0)
    gk_v[...] = grad[:, 0:256].astype(BF16)
    gv_v[...] = grad[:, 256:512].astype(BF16)

    for li in range(4):
        shape = ret.at[pl.ds(64 * min(li, 2), 64)] if li < 3 else ret5
        wait_bytes(shape, pool_send.at[li])
        wait_bytes(shape, ret_send.at[li])
        fwds[li].wait_send()
    near_p.wait_send()
    near_o.wait_send()
    wait_bytes(ps_buf, ps_sem.at[0])
    swap.wait_send()
    swap_far.wait_send()
    rim_p.wait_send()
    rim_o.wait_send()


def store(a, b, c, e, a_hbm, b_hbm, c_hbm, e_hbm, sem):
    copies = [
        pltpu.make_async_copy(src, dst_ref, sem.at[i])
        for i, (src, dst_ref) in enumerate(((a, a_hbm), (b, b_hbm), (c, c_hbm), (e, e_hbm)))
    ]
    for copy in copies:
        copy.start()
    for copy in copies:
        copy.wait()


def solution(mesh):
    n_ctx, n_head = mesh.shape["ctx"], mesh.shape["head"]
    hbm = pl.BlockSpec(memory_space=pl.ANY)
    vmem = pl.BlockSpec(memory_space=pltpu.VMEM)
    dma = pltpu.SemaphoreType.DMA

    def body(queries, keys, values, near_blocks, near_count, head_scale, gain, cotangent):
        out = jax.ShapeDtypeStruct((TOK, 256), BF16)
        outs = pl.pallas_call(
            functools.partial(kernel, n_ctx, n_head),
            out_shape=(pltpu.VMEM((TOK, 256), BF16),) * 4,
            in_specs=[hbm] * 8,
            out_specs=(vmem, vmem, vmem, vmem),
            scratch_shapes=[
                pltpu.SMEM((2, SLOTS), jnp.int32),
                pltpu.SMEM((2,), jnp.int32),
                pltpu.SMEM((2,), F32),
                pltpu.VMEM((256,), F32),
                pltpu.VMEM((ROWS, COLS), BF16),
                pltpu.VMEM((TOK, 256), BF16),
                pltpu.VMEM((TOK, 256), BF16),
                pltpu.VMEM((112, COLS), BF16),
                pltpu.VMEM((16, 256), BF16),
                pltpu.VMEM((16, 16, 256), BF16),
                pltpu.VMEM((2, TOK), F32),
                pltpu.VMEM((n_head - 1, 2, TOK), F32),
                pltpu.VMEM((COARSE, TOK), F32),
                pltpu.VMEM((256, TOK), F32),
                pltpu.VMEM((2, ROWS, TOK), BF16),
                pltpu.VMEM((2, ROWS, TOK), BF16),
                pltpu.VMEM((COARSE, COLS), F32),
                pltpu.VMEM((512, COLS), F32),
                pltpu.VMEM((256, COLS), BF16),
                pltpu.VMEM((256, COLS), BF16),
                pltpu.VMEM((2, TOK, COLS), BF16),
                pltpu.VMEM((2, TOK, COLS), BF16),
                pltpu.VMEM((192, COLS), BF16),
                pltpu.VMEM((8, 16, 256), BF16),
                pltpu.VMEM((192, COLS), BF16),
                pltpu.VMEM((8, 16, 256), BF16),
                pltpu.VMEM((TOK, COLS), F32),
                dma((8,)), dma((4,)), dma((4,)), dma((4,)), dma((4,)),
                dma((2,)), dma((2,)), dma((2,)), dma((4,)), dma((2,)), dma((2,)),
                dma((4,)), dma((4,)),
            ],
            compiler_params=pltpu.CompilerParams(
                collective_id=0, has_side_effects=True, vmem_limit_bytes=56 * 1024 * 1024
            ),
        )(queries, keys, values, near_blocks, near_count, head_scale, gain, cotangent)
        return pl.pallas_call(
            store,
            out_shape=(out, out, out, out),
            in_specs=[hbm] * 4,
            out_specs=(hbm, hbm, hbm, hbm),
            scratch_shapes=[dma((4,))],
            compiler_params=pltpu.CompilerParams(vmem_limit_bytes=1024 * 1024),
        )(*outs)

    return jax.shard_map(
        body,
        mesh=mesh,
        in_specs=(
            P("ctx", "head"), P("ctx", "head"), P("ctx", "head"), P("ctx", None),
            P("ctx"), P("head"), P("head"), P("ctx", "head"),
        ),
        out_specs=(P("ctx", "head"), P("ctx", "head"), P("ctx", "head"), P("ctx", "head")),
        check_vma=False,
    )
```

```python
import functools
import math

import jax
import jax.numpy as jnp
from jax import lax
from jax.experimental import pallas as pl
from jax.experimental.pallas import tpu as pltpu
from jax.sharding import PartitionSpec as P

HS = 128
BT = 128
SLOTS = 4
NEG_BIG = -1e30
NORM_EPS = 1e-05
LOG2E = 1.4426950408889634
SCALE = 1.0 / math.sqrt(HS)
TOK = 256
COLS = 512
NEAR = 768
ROWS = 1408
COARSE = ROWS - NEAR
F32 = jnp.float32
BF16 = jnp.bfloat16


def dot(a, b, ca, cb):
    return lax.dot_general(
        a, b, (((ca,), (cb,)), ((), ())), preferred_element_type=F32
    )


def iota(shape, dim):
    return lax.broadcasted_iota(jnp.int32, shape, dim)


def pool_matrix(rows, level):
    hit = (iota((rows, TOK), 1) >> level) == iota((rows, TOK), 0)
    return jnp.where(hit, 2.0**-level, 0.0)


def kernel(
    n_ctx, n_head,
    q_hbm, k_hbm, v_hbm, nb_hbm, nc_hbm, hs_hbm, gain_hbm, cot_hbm,
    mixed_v, gq_v, gk_v, gv_v,
    nb_ref, nc_ref, hs_ref, gain_v,
    kall, qv, cotv, pool, pool5, buf5, ps_own, ps_buf, cbias, back,
    pt, dst, cg, ext, c_send, c_recv, rim_out, rim_in, csum, csum5, ret, ret5, ext_o,
    ld_sem, pool_send, pool_recv, fwd_send, fwd_recv, near_send, near_recv,
    ps_sem, cp_sem, rim_send, rim_recv, ret_send, ret_recv,
):
    d = lax.axis_index("ctx")
    z = lax.axis_index("head")
    n_chip = n_ctx // 2
    chip = lax.div(d, 2)
    core = lax.rem(d, 2)
    across = 1 - core
    partner = chip * 2 + across
    other = lax.rem(d + n_ctx - 1 + 2 * core, n_ctx)
    width = float(n_head * 2 * HS)

    barrier = pltpu.get_barrier_semaphore()

    def hello(ctx, head):
        pl.semaphore_signal(
            barrier, inc=1, device_id=(ctx, head), device_id_type=pl.DeviceIdType.MESH
        )

    def remote(src, dst_ref, ssem, rsem, ctx, head):
        return pltpu.make_async_remote_copy(
            src_ref=src, dst_ref=dst_ref, send_sem=ssem, recv_sem=rsem,
            device_id=(ctx, head), device_id_type=pl.DeviceIdType.MESH,
        )

    def wait_bytes(ref, sem):
        pltpu.make_async_copy(ref, ref, sem).wait()

    loads = [
        pltpu.make_async_copy(k_hbm, kall.at[pl.ds(TOK, TOK), pl.ds(0, 256)], ld_sem.at[0]),
        pltpu.make_async_copy(v_hbm, kall.at[pl.ds(TOK, TOK), pl.ds(256, 256)], ld_sem.at[1]),
        pltpu.make_async_copy(q_hbm, qv, ld_sem.at[2]),
        pltpu.make_async_copy(cot_hbm, cotv, ld_sem.at[3]),
        pltpu.make_async_copy(gain_hbm, gain_v, ld_sem.at[4]),
        pltpu.make_async_copy(nb_hbm, nb_ref, ld_sem.at[5]),
        pltpu.make_async_copy(nc_hbm, nc_ref, ld_sem.at[6]),
        pltpu.make_async_copy(hs_hbm, hs_ref, ld_sem.at[7]),
    ]
    for load in loads:
        load.start()
    for m in range(1, n_chip):
        hello(lax.rem(chip + m, n_chip) * 2 + across, z)
    hello(partner, z)
    for m in range(1, n_head):
        hello(d, lax.rem(z + m, n_head))

    pm = jnp.concatenate(
        [pool_matrix(64, 2), pool_matrix(32, 3), pool_matrix(16, 4), pool_matrix(8, 5),
         jnp.zeros((8, TOK), F32)], axis=0,
    ).astype(BF16)
    loads[0].wait()
    loads[1].wait()
    pooled = dot(pm, kall[TOK : 2 * TOK, :], 1, 0)
    pool[...] = pooled[0:112].astype(BF16)
    pool5[...] = jnp.concatenate([pooled[112:120, 0:256], pooled[112:120, 256:512]], axis=0).astype(BF16)

    pl.semaphore_wait(barrier, n_head - 1 + n_chip - 1 + 1)

    def level_peers(li):
        c = 1 << li
        half = lax.div(chip, c)
        base = (half + 1 - 2 * lax.rem(half, 2)) * c
        return c, 64 >> li, base, lax.rem(chip, c)

    pool_off = (0, 64, 96)
    for li in (3, 2, 1, 0):
        c, n, base, pos = level_peers(li)
        for j in range(c):
            if li < 3:
                src = pool.at[pl.ds(pool_off[li], n)]
                row = pl.multiple_of(NEAR + 128 * (li + 1) + core * 64 + pos * n, 16)
                dst_ref = kall.at[pl.ds(row, n)]
            else:
                src = pool5
                dst_ref = buf5.at[core * 8 + pos]
            remote(src, dst_ref, pool_send.at[li], pool_recv.at[li], (base + j) * 2 + across, z).start()

    own = kall.at[pl.ds(TOK, TOK)]
    near_p = remote(
        own, kall.at[pl.ds(pl.multiple_of(core * 512, 256), TOK)],
        near_send.at[0], near_recv.at[0], partner, z,
    )
    near_o = remote(
        own, kall.at[pl.ds(pl.multiple_of((1 - core) * 512, 256), TOK)],
        near_send.at[1], near_recv.at[1], other, z,
    )
    near_p.start()

    qb = lax.div(iota((128, TOK), 1), 128) + 2 * d
    r = iota((128, TOK), 0)
    kb = 2 * partner + (r >> 6)
    cbias[0:128] = jnp.where(jnp.abs(kb - qb) > 2, 1.0, NEG_BIG)
    for li in range(4):
        c, n, base, pos = level_peers(li)
        rr = r & 63
        chips = base + (rr >> (6 - li))
        first = (chips * 2 + (r >> 6)) * TOK + (rr & (n - 1)) * (4 << li)
        cbias[128 * (li + 1) : 128 * (li + 2)] = jnp.where(
            jnp.abs((first >> 7) - qb) > 2, float(li + 2), NEG_BIG
        )
    near_o.start()
    loads[3].wait()
    loads[4].wait()
    gain = gain_v[...].reshape(1, 256)
    back[...] = (cotv[...].astype(F32) * gain).T
    for load in loads[5:]:
        load.wait()
    loads[2].wait()

    def half_ref(li, which):
        if li < 3:
            row = pl.multiple_of(NEAR + 128 * (li + 1) + which * 64, 64)
            return kall.at[pl.ds(row, 64)]
        return buf5.at[pl.ds(which * 8, 8)]

    def kcols(h):
        return slice(h * HS, (h + 1) * HS)

    def vcols(h):
        return slice(256 + h * HS, 256 + (h + 1) * HS)

    local = pl.ds(pl.multiple_of(across * 256, 256), 512)
    beside = pl.ds(pl.multiple_of(core * 512, 256), 256)
    far = pl.ds(NEAR, COARSE)

    def group(h, rows, bias):
        s = dot(kall[rows, kcols(h)], qv[:, kcols(h)], 1, 1) * (SCALE * LOG2E) + bias
        top = jnp.max(s, axis=0, keepdims=True)
        p = jnp.exp2(s - top)
        total = jnp.sum(p, axis=0, keepdims=True)
        pb = p.astype(BF16)
        pt[h, rows, :] = pb
        out = dot(kall[rows, vcols(h)], pb, 0, 0)
        return top, total, out

    lane_block = lax.div(iota((1, TOK), 1), 128)

    def list_bias(first, count):
        rows_bias = []
        for e in range(count):
            vals = []
            for i in range(2):
                hit = jnp.int32(0)
                for j in range(SLOTS):
                    ok = jnp.where(nb_ref[i, j] == first + e, 1, 0) * jnp.where(nc_ref[i] > j, 1, 0)
                    hit = jnp.maximum(hit, ok)
                vals.append(jnp.where(hit > 0, 0.0, NEG_BIG))
            row = jnp.where(lane_block == 0, vals[0], vals[1])
            rows_bias.append(jnp.broadcast_to(row, (128, TOK)))
        return jnp.concatenate(rows_bias, axis=0)

    near_p.wait_recv()
    local_bias = list_bias(2 * d - 2 + 2 * across, 4)
    inner = [group(h, local, local_bias) for h in range(2)]

    p1 = pool_matrix(128, 1).astype(BF16)
    part = kall[pl.ds(pl.multiple_of(across * 512, 256), TOK), :]
    kall[NEAR : NEAR + 128, :] = dot(p1, part, 1, 0).astype(BF16)

    fwds = [None] * 4

    def relay(li):
        mine = half_ref(li, across)
        wait_bytes(mine, pool_recv.at[li])
        fwds[li] = remote(mine, mine, fwd_send.at[li], fwd_recv.at[li], partner, z)
        fwds[li].start()

    for li in range(4):
        relay(li)
    for li in range(4):
        fwds[li].wait_recv()
    five = buf5[...].astype(F32)
    kall[ROWS - 128 : ROWS, 0:256] = five[:, 0:8, :].reshape(128, 256).astype(BF16)
    kall[ROWS - 128 : ROWS, 256:512] = five[:, 8:16, :].reshape(128, 256).astype(BF16)

    coarse = [group(h, far, cbias[...]) for h in range(2)]

    near_o.wait_recv()
    beside_bias = list_bias(2 * d - 2 + 4 * core, 2)
    outer = [group(h, beside, beside_bias) for h in range(2)]

    attn, alphas, scaled = [], [], []
    usum = jnp.zeros((1, TOK), F32)
    vsum = jnp.zeros((1, TOK), F32)
    for h in range(2):
        parts = (coarse[h], inner[h], outer[h])
        top = functools.reduce(jnp.maximum, [part[0] for part in parts])
        factors = [jnp.exp2(part[0] - top) for part in parts]
        inv_total = 1.0 / sum(f * part[1] for f, part in zip(factors, parts))
        factors = [f * inv_total for f in factors]
        out = sum(f * part[2] for f, part in zip(factors, parts))
        sc = out * hs_ref[h]
        usum = usum + jnp.sum(sc * sc, axis=0, keepdims=True)
        vsum = vsum + jnp.sum(sc * back[kcols(h), :], axis=0, keepdims=True)
        attn.append(out)
        alphas.append(factors)
        scaled.append(sc)
    ps_own[0:1, :] = usum
    ps_own[1:2, :] = vsum
    for m in sorted(range(1, n_head), key=lambda m: -min(m, n_head - m)):
        remote(
            ps_own, ps_buf.at[m - 1], ps_sem.at[0], ps_sem.at[1], d, lax.rem(z + m, n_head)
        ).start()

    u = iota((TOK, TOK), 0)
    col = iota((TOK, TOK), 1)
    lvl = (col >> 6) + 2
    rel = (col & 63) & ((256 >> lvl) - 1)
    spread = jnp.where(
        (u >> lvl) == rel,
        jnp.where(lvl == 2, 0.25, jnp.where(lvl == 3, 0.125, jnp.where(lvl == 4, 0.0625, 0.03125))),
        0.0,
    ).astype(BF16)
    e1 = jnp.where(
        (iota((TOK, 128), 0) >> 1) == iota((TOK, 128), 1), 0.5, 0.0
    ).astype(BF16)

    wait_bytes(ps_buf, ps_sem.at[1])
    sums = ps_own[...] + jnp.sum(ps_buf[...], axis=0)
    inv = lax.rsqrt(sums[0:1, :] / width + NORM_EPS)
    fac = inv * inv * (sums[1:2, :] / width)

    d_group = []
    for h in range(2):
        d_attn = (inv * hs_ref[h]) * (back[kcols(h), :] - scaled[h] * fac)
        d_group.append([(d_attn * a).astype(BF16) for a in alphas[h]])

    def backward(h, g, rows, keep, to=slice(None)):
        dg = d_group[h][g]
        delta = jnp.sum(dg.astype(F32) * attn[h], axis=0, keepdims=True)
        dp = dot(kall[rows, vcols(h)], dg, 1, 0)
        pg = pt[h, rows, :]
        ds = (pg.astype(F32) * (dp - delta)).astype(BF16)
        dst[h, rows, :] = ds
        keep[to, kcols(h)] = dot(ds, qv[:, kcols(h)], 1, 0) * SCALE
        keep[to, vcols(h)] = dot(pg, dg, 1, 1)

    for h in range(2):
        backward(h, 2, beside, ext_o)
    rim_out[1] = ext_o[...].astype(BF16)
    rim_o = remote(rim_out.at[1], rim_in.at[1], rim_send.at[1], rim_recv.at[1], other, z)
    rim_o.start()
    for h in range(2):
        backward(h, 0, pl.ds(NEAR + 384, 256), cg, slice(384, 640))

    def start_swap(lis, i):
        for li in lis:
            row = pl.multiple_of(128 * (li + 1) + core * 64, 64)
            c_send[64 * li : 64 * (li + 1), :] = cg[pl.ds(row, 64), :].astype(BF16)
        half = pl.ds(64 * lis[0], 128)
        copy = remote(c_send.at[half], c_recv.at[half], cp_sem.at[i], cp_sem.at[2 + i], partner, z)
        copy.start()
        return copy

    swap_far = start_swap((2, 3), 0)
    for h in range(2):
        backward(h, 0, pl.ds(NEAR, 384), cg, slice(0, 384))
    swap = start_swap((0, 1), 1)

    swap_far.wait_recv()
    for li in (3, 2, 1, 0):
        if li == 1:
            backward(0, 1, local, ext)
            swap.wait_recv()
        row = pl.multiple_of(128 * (li + 1) + across * 64, 64)
        total = cg[pl.ds(row, 64), :] + c_recv[64 * li : 64 * (li + 1), :].astype(F32)
        if li < 3:
            csum[64 * li : 64 * (li + 1), :] = total.astype(BF16)
        else:
            csum5[...] = jnp.concatenate(
                [total[:, 0:256].reshape(8, 8, 256), total[:, 256:512].reshape(8, 8, 256)], axis=1
            ).astype(BF16)
        c, n, base, pos = level_peers(li)
        for j in range(c):
            if li < 3:
                src = csum.at[pl.ds(64 * li + j * n, n)]
                dst_ref = ret.at[pl.ds(pl.multiple_of(64 * li + pos * n, 16), n)]
            else:
                src = csum5.at[j]
                dst_ref = ret5.at[pos]
            remote(src, dst_ref, ret_send.at[li], ret_recv.at[li], (base + j) * 2 + across, z).start()

    backward(1, 1, local, ext)
    rim_out[0] = (
        ext[pl.ds(pl.multiple_of(across * 256, 256), TOK), :]
        + dot(e1, cg[0:128, :].astype(BF16), 1, 0)
    ).astype(BF16)
    rim_p = remote(rim_out.at[0], rim_in.at[0], rim_send.at[0], rim_recv.at[0], partner, z)
    rim_p.start()

    for h in range(2):
        mixed_v[:, kcols(h)] = ((scaled[h] * inv).T * gain[:, kcols(h)]).astype(BF16)
    for h in range(2):
        gqt = dot(kall[:, kcols(h)], dst[h], 0, 0) * SCALE
        gq_v[:, kcols(h)] = gqt.T.astype(BF16)

    rim_p.wait_recv()
    rim_o.wait_recv()
    grad = ext[pl.ds(pl.multiple_of(core * 256, 256), TOK), :] + rim_in[0].astype(F32) + rim_in[1].astype(F32)
    for li in range(3):
        wait_bytes(ret.at[pl.ds(64 * li, 64)], ret_recv.at[li])
    wait_bytes(ret5, ret_recv.at[3])
    last = ret5[...].astype(F32)
    last = jnp.concatenate(
        [last[:, 0:8, :].reshape(64, 256), last[:, 8:16, :].reshape(64, 256)], axis=1
    ).astype(BF16)
    whole = jnp.concatenate([ret[...], last], axis=0)
    grad = grad + dot(spread, whole, 1, 0)
    gk_v[...] = grad[:, 0:256].astype(BF16)
    gv_v[...] = grad[:, 256:512].astype(BF16)

    for li in range(4):
        shape = ret.at[pl.ds(64 * min(li, 2), 64)] if li < 3 else ret5
        wait_bytes(shape, pool_send.at[li])
        wait_bytes(shape, ret_send.at[li])
        fwds[li].wait_send()
    near_p.wait_send()
    near_o.wait_send()
    wait_bytes(ps_buf, ps_sem.at[0])
    swap.wait_send()
    swap_far.wait_send()
    rim_p.wait_send()
    rim_o.wait_send()


def store(a, b, c, e, a_hbm, b_hbm, c_hbm, e_hbm, sem):
    copies = [
        pltpu.make_async_copy(src, dst_ref, sem.at[i])
        for i, (src, dst_ref) in enumerate(((a, a_hbm), (b, b_hbm), (c, c_hbm), (e, e_hbm)))
    ]
    for copy in copies:
        copy.start()
    for copy in copies:
        copy.wait()


def solution(mesh):
    n_ctx, n_head = mesh.shape["ctx"], mesh.shape["head"]
    hbm = pl.BlockSpec(memory_space=pl.ANY)
    vmem = pl.BlockSpec(memory_space=pltpu.VMEM)
    dma = pltpu.SemaphoreType.DMA

    def body(queries, keys, values, near_blocks, near_count, head_scale, gain, cotangent):
        out = jax.ShapeDtypeStruct((TOK, 256), BF16)
        outs = pl.pallas_call(
            functools.partial(kernel, n_ctx, n_head),
            out_shape=(pltpu.VMEM((TOK, 256), BF16),) * 4,
            in_specs=[hbm] * 8,
            out_specs=(vmem, vmem, vmem, vmem),
            scratch_shapes=[
                pltpu.SMEM((2, SLOTS), jnp.int32),
                pltpu.SMEM((2,), jnp.int32),
                pltpu.SMEM((2,), F32),
                pltpu.VMEM((256,), F32),
                pltpu.VMEM((ROWS, COLS), BF16),
                pltpu.VMEM((TOK, 256), BF16),
                pltpu.VMEM((TOK, 256), BF16),
                pltpu.VMEM((112, COLS), BF16),
                pltpu.VMEM((16, 256), BF16),
                pltpu.VMEM((16, 16, 256), BF16),
                pltpu.VMEM((2, TOK), F32),
                pltpu.VMEM((n_head - 1, 2, TOK), F32),
                pltpu.VMEM((COARSE, TOK), F32),
                pltpu.VMEM((256, TOK), F32),
                pltpu.VMEM((2, ROWS, TOK), BF16),
                pltpu.VMEM((2, ROWS, TOK), BF16),
                pltpu.VMEM((COARSE, COLS), F32),
                pltpu.VMEM((512, COLS), F32),
                pltpu.VMEM((256, COLS), BF16),
                pltpu.VMEM((256, COLS), BF16),
                pltpu.VMEM((2, TOK, COLS), BF16),
                pltpu.VMEM((2, TOK, COLS), BF16),
                pltpu.VMEM((192, COLS), BF16),
                pltpu.VMEM((8, 16, 256), BF16),
                pltpu.VMEM((192, COLS), BF16),
                pltpu.VMEM((8, 16, 256), BF16),
                pltpu.VMEM((TOK, COLS), F32),
                dma((8,)), dma((4,)), dma((4,)), dma((4,)), dma((4,)),
                dma((2,)), dma((2,)), dma((2,)), dma((4,)), dma((2,)), dma((2,)),
                dma((4,)), dma((4,)),
            ],
            compiler_params=pltpu.CompilerParams(
                collective_id=0, has_side_effects=True, vmem_limit_bytes=56 * 1024 * 1024
            ),
        )(queries, keys, values, near_blocks, near_count, head_scale, gain, cotangent)
        return pl.pallas_call(
            store,
            out_shape=(out, out, out, out),
            in_specs=[hbm] * 4,
            out_specs=(hbm, hbm, hbm, hbm),
            scratch_shapes=[dma((4,))],
            compiler_params=pltpu.CompilerParams(vmem_limit_bytes=1024 * 1024),
        )(*outs)

    return jax.shard_map(
        body,
        mesh=mesh,
        in_specs=(
            P("ctx", "head"), P("ctx", "head"), P("ctx", "head"), P("ctx", None),
            P("ctx"), P("head"), P("head"), P("ctx", "head"),
        ),
        out_specs=(P("ctx", "head"), P("ctx", "head"), P("ctx", "head"), P("ctx", "head")),
        check_vma=False,
    )
```
